512 devices in a mesh: seq: 16 (over z, core), batch: 16 (over y_lo, x), tp: 2 (over y_hi).
Axes of the slice: x: 4, y: 8 (y_hi: 2, y_lo: 4; y = y_hi * 4 + y_lo), z: 8, core: 2. Of those that a mesh axis runs over, the one named last changes fastest.
Arguments:
- pre_q: bfloat16 [16, 2048, 4096], P('batch', 'seq', 'tp'), may hold values from -40 to 40
- pre_k: bfloat16 [16, 2048, 512], P('batch', 'seq', 'tp'), may hold values from -40 to 40
- pre_v: bfloat16 [16, 2048, 512], P('batch', 'seq', 'tp'), may hold values from -12 to 12
- owner_map: int32 [16, 128, 1], P('batch', 'seq'), may hold values from 0 to 15; in each aligned block of 8 rows (0 to 7, 8 to 15, ..., all dimensions but the last counted through in order) at most 2 rows name the same one
- cache_k: bfloat16 [128, 256, 512], P('batch', 'seq', 'tp'), may hold values from -6 to 6
- cache_v: bfloat16 [128, 256, 512], P('batch', 'seq', 'tp'), may hold values from -12 to 12
- tables: int32 [32, 64], P('batch', 'seq'), may hold values from 0 to 7, as said below
- lengths: int32 [32], P('batch'), may hold values from 1 to 1024, 16384 in all
- dec_q: float32 [32, 3, 4096], P('batch', None, 'tp'), may hold values from -40 to 40
- dec_k: float32 [32, 3, 512], P('batch', None, 'tp'), may hold values from -40 to 40
- dec_v: float32 [32, 3, 512], P('batch', None, 'tp'), may hold values from -12 to 12
- w_out: bfloat16 [4096, 8192], P('tp', 'seq'), may hold values from -0.09375 to 0.09375
Outputs:
- pre_out: bfloat16 [16, 2048, 4096], P('batch', 'seq', 'tp')
- dec_out: float32 [32, 3, 8192], P('batch', None, 'seq')
The draws below stay inside these ranges and needn't reach their ends.
Inputs may be any that keep to these rules, and one draw needn't show every extreme that they name: `owner_map`: in each aligned block of 8 rows (the pages of one index of seq of one span) no owner is named more than 2 times. `tables`: within one owner's 2 requests and one index of seq, the 8 entries are distinct.
All inputs are finite; a program needn't handle non-finite values. No bound on the sum of `lengths` on one device may be relied on, other than what follows from the above.
Results may differ from the reference program's by a relative error of at most 0.0033.
Values may be sent and summed in bfloat16 or wider, within the bound.
No kernel may reach another device: no remote copies, remote signals or barrier semaphores. Data moves between devices by JAX's collectives and lax.ppermute only.
A program may use at most 64 MiB of HBM per device.

```python
import math
import jax
import jax.numpy as jnp
import numpy as np
from jax import lax

HD = 128
QH = 32
KVH = 4
D = 8192
PAGE = 16
NEW = 3
R_DEV = 2
TBL = 4
SEQ_LEN = 2048
PG_DEV = 8
MOST = 2
REQS = 32
POOL = 8
CTX = 1024
N_SEQ = 16
N_BATCH = 16


def draw_pre_k(key, part):
    key = jax.random.fold_in(key, 21)
    return jnp.clip(jax.random.normal(key, (N_BATCH, SEQ_LEN, KVH * HD), jnp.float32), -5.0, 5.0).astype(jnp.bfloat16)


def draw_pre_q(key, part):
    key = jax.random.fold_in(key, 22)
    return (2.0 * jnp.clip(jax.random.normal(key, (N_BATCH, SEQ_LEN, QH * HD), jnp.float32), -5.0, 5.0)).astype(jnp.bfloat16)


def draw_dec_k(key, part):
    key = jax.random.fold_in(key, 31)
    return jnp.clip(jax.random.normal(key, (REQS, NEW, KVH * HD), jnp.float32), -5.0, 5.0)


def draw_dec_q(key, part):
    key = jax.random.fold_in(key, 32)
    return 2.0 * jnp.clip(jax.random.normal(key, (REQS, NEW, QH * HD), jnp.float32), -5.0, 5.0)


def draw_tables(key, part):
    key = jax.random.fold_in(key, 5)
    split_keys = jax.random.split(key, N_BATCH * N_SEQ)
    orders = jax.vmap(lambda single: jax.random.permutation(single, POOL))(split_keys).astype(jnp.int32)
    orders = orders.reshape(N_BATCH, N_SEQ, R_DEV, TBL).transpose(0, 2, 1, 3)
    return orders.reshape(REQS, N_SEQ * TBL)


def block_scale(key, shape, shards, low, high):
    def one(axis_at, blocks):
        steps = jax.random.uniform(jax.random.fold_in(jax.random.fold_in(key, 6), axis_at), (blocks,), jnp.float32, low / len(shards), high / len(shards))
        return jnp.repeat(jnp.exp(steps), shape[axis_at] // blocks).reshape((-1,) + (1,) * (len(shape) - axis_at - 1))

    factor_of = one(*shards[0])
    for cut in shards[1:]:
        factor_of = factor_of * one(*cut)
    return factor_of


def profile(count, total, reach, slope):
    portions = [(1 << 20) // math.isqrt(grade ** slope) + 1 for grade in range(2, count + 1)]
    rest, holding = total - reach - (count - 1), [1] * (count - 1)
    while rest > 0:
        candidates = [i for i in range(count - 1) if holding[i] < reach]
        whole, budget = sum([portions[i] for i in candidates]), rest
        for i in candidates:
            more = min(reach - holding[i], max(1, budget * portions[i] // whole), rest)
            holding[i] = holding[i] + more
            rest = rest - more
    return np.array([reach] + holding)


def ragged_sizes(stream_key, count, total, most, lean):
    if count == 2:
        one = jax.random.randint(stream_key, (), max(1, total - most), min(most, total - 1) + 1)
        return jnp.stack([one, total - one])
    sizes = jnp.asarray(profile(count, total, most, lean), jnp.int32)
    couples = (count - 1) // 2
    donor, receiver = sizes[1:1 + 2 * couples:2], sizes[2:2 + 2 * couples:2]
    room = jnp.minimum(donor - 1, most - receiver)
    moved = jax.random.randint(jax.random.fold_in(stream_key, 1), (couples,), 0, 1 << 20) % (room + 1)
    sizes = sizes.at[1:1 + 2 * couples:2].set(donor - moved).at[2:2 + 2 * couples:2].set(receiver + moved)
    return sizes[jax.random.permutation(jax.random.fold_in(stream_key, 2), count)]


def shared_out(rng, own, number, rows, number_of, top, most, skew):
    sequence = jax.random.permutation(rng, number_of)
    crowded, usual = load_shares(number_of, rows * top, most, skew, True), load_shares(number_of, rows * top, most, skew, False)
    places = jnp.arange(number_of)

    def named(sizes, rotation):
        used = int((sizes > 0).sum())
        fixed = max(1, used // 4)
        passed = fixed + (places - fixed + rotation * (used - fixed)) % max(1, number_of - fixed)
        return jnp.zeros((number_of,), jnp.int32).at[sequence[jnp.where(places < fixed, places, passed)]].set(jnp.asarray(sizes, jnp.int32))

    sizes = jnp.where(number % 4 == 0, named(crowded, number // 4), named(usual, number - number // 4 - 1))
    mixed = jax.random.permutation(jax.random.fold_in(own, 3), number_of)
    donor, sink = mixed[0:number_of // 2 * 2:2], mixed[1:number_of // 2 * 2:2]
    room = jnp.minimum(sizes[donor] - 1, most - sizes[sink]) // 2
    room = jnp.where((donor == sequence[0]) | (sink == sequence[0]) | (sizes[sink] == 0), 0, jnp.maximum(room, 0))
    passed = jax.random.randint(jax.random.fold_in(own, 4), (number_of // 2,), 0, 1 << 20) % (room + 1)
    sizes = sizes.at[donor].add(-passed).at[sink].add(passed)
    labels = jnp.searchsorted(jnp.cumsum(sizes), jnp.arange(rows * top), side="right").astype(jnp.int32)
    grid = labels.reshape(top, rows).T
    grid = grid[jax.random.permutation(jax.random.fold_in(own, 1), rows)]
    rotation = jax.random.randint(jax.random.fold_in(own, 2), (rows, 1), 0, top)
    return jnp.take_along_axis(grid, (jnp.arange(top)[None, :] + rotation) % top, axis=1)


def load_shares(number_of, total, most, lean, full):
    portions = [(1 << 20) // math.isqrt(rank ** lean) + 1 for rank in range(1, number_of + 1)]
    largest = most if full else min(most, max(-(-total // number_of), total * portions[0] // sum(portions)))
    least = 1 if total - largest >= number_of - 1 else 0
    counts, rest = [largest] + [least] * (number_of - 1), total - largest - least * (number_of - 1)
    while rest > 0:
        free = [i for i in range(1, number_of) if counts[i] < largest] or [i for i in range(1, number_of) if counts[i] < most]
        whole, left = sum([portions[i] for i in free]), rest
        for i in free:
            addition = min(most - counts[i], max(1, left * portions[i] // whole), rest)
            counts[i] = counts[i] + addition
            rest = rest - addition
    return np.array(counts)


def normal_values(stream_key, dims, spread, reach, shards=(), held_as=jnp.bfloat16):
    result = jax.random.normal(stream_key, dims, jnp.float32) * spread
    if len(shards) > 0:
        result = block_scale(stream_key, dims, shards, -0.22, 0.18) * result
    return jnp.clip(result, min=-reach, max=reach).astype(held_as)


def setup_inputs(seed: int = 0) -> dict:
    keys = jax.random.split(jax.random.key(seed), 13)
    pre_q = draw_pre_q(jax.random.fold_in(keys[12], 71), 0)
    pre_k = draw_pre_k(jax.random.fold_in(keys[12], 71), 0)
    pre_v = normal_values(keys[2], (N_BATCH, SEQ_LEN, KVH * HD), 2.0, 12.0, ((0, 16), (1, 16), (2, 2)))
    owner_map_keys = jax.random.split(jax.random.fold_in(keys[3], 1), N_BATCH * (N_SEQ * PG_DEV) // PG_DEV)
    owner_map_turns = jax.random.permutation(jax.random.fold_in(keys[3], 3), N_BATCH * (N_SEQ * PG_DEV) // PG_DEV)
    owner_map = jax.vmap(lambda own, number: shared_out(jax.random.fold_in(keys[3], 2), own, number, PG_DEV, N_BATCH, 1, MOST, 2))(owner_map_keys, owner_map_turns).reshape((N_BATCH, N_SEQ * PG_DEV, 1))
    cache_k = normal_values(keys[4], (REQS * TBL, N_SEQ * PAGE, KVH * HD), 1.0, 6.0, ((0, 16), (1, 16), (2, 2)))
    cache_v = normal_values(keys[5], (REQS * TBL, N_SEQ * PAGE, KVH * HD), 2.0, 12.0, ((0, 16), (1, 16), (2, 2)))
    tables = draw_tables(jax.random.fold_in(keys[12], 71), 0)
    lengths = ragged_sizes(keys[7], REQS, REQS * CTX // 2, CTX, 2).astype(jnp.int32)
    dec_q = draw_dec_q(jax.random.fold_in(keys[12], 71), 0)
    dec_k = draw_dec_k(jax.random.fold_in(keys[12], 71), 0)
    dec_v = normal_values(keys[10], (REQS, NEW, KVH * HD), 2.0, 12.0, ((0, 16), (2, 2)), jnp.float32)
    w_out = normal_values(keys[11], (QH * HD, D), (QH * HD) ** -0.5, 0.09375, ((0, 2), (1, 16)))
    return dict(pre_q=pre_q, pre_k=pre_k, pre_v=pre_v, owner_map=owner_map, cache_k=cache_k, cache_v=cache_v, tables=tables, lengths=lengths, dec_q=dec_q, dec_k=dec_k, dec_v=dec_v, w_out=w_out)


highest = lax.Precision.HIGHEST
floor_score = -1e30


def prefill_span(inputs):
    queries, key_rows, value_rows = inputs
    group_size = QH // KVH
    scaling = HD ** -0.5
    q_all = queries.astype(jnp.float32).reshape(SEQ_LEN, KVH, group_size, HD)
    k_all = key_rows.astype(jnp.float32).reshape(SEQ_LEN, KVH, HD)
    v_all = value_rows.astype(jnp.float32).reshape(SEQ_LEN, KVH, HD)
    block_rows = min(512, SEQ_LEN)
    pieces = []
    for block_id in range(SEQ_LEN // block_rows):
        end_row = (block_id + 1) * block_rows
        query_block = q_all[block_id * block_rows:end_row]
        scores = jnp.einsum("qkgd,skd->kgqs", query_block, k_all[:end_row], precision=highest) * scaling
        query_pos = block_id * block_rows + jnp.arange(block_rows, dtype=jnp.int32)
        visible = jnp.arange(end_row, dtype=jnp.int32)[None, :] <= query_pos[:, None]
        masked = jnp.where(visible, scores, floor_score)
        row_peak = jnp.max(masked, axis=-1, keepdims=True)
        weights = jnp.where(visible, jnp.exp(scores - row_peak), 0.0)
        row_total = jnp.sum(weights, axis=-1)
        rounded = lax.optimization_barrier(weights.astype(jnp.bfloat16)).astype(jnp.float32)
        mixture = jnp.einsum("kgqs,skd->qkgd", rounded, v_all[:end_row], precision=highest)
        mixture = mixture / jnp.transpose(row_total, (2, 0, 1))[..., None]
        pieces.append(mixture.reshape(block_rows, QH * HD).astype(jnp.bfloat16))
    return jnp.concatenate(pieces, axis=0)


def reference(pre_q, pre_k, pre_v, owner_map, cache_k, cache_v, tables, lengths, dec_q, dec_k, dec_v, w_out):
    pre_out = lax.map(prefill_span, (pre_q, pre_k, pre_v))
    group_size = QH // KVH
    scaling = HD ** -0.5
    token_keys = pre_k.reshape(N_BATCH * SEQ_LEN, KVH, HD)
    token_values = pre_v.reshape(N_BATCH * SEQ_LEN, KVH, HD)
    token_owner = jnp.repeat(owner_map.reshape(-1), PAGE).astype(jnp.int32)
    capacity = min(N_BATCH * SEQ_LEN, N_BATCH * N_SEQ * MOST * PAGE)
    positions = ((jnp.arange(TBL, dtype=jnp.int32)[None, :, None] * N_SEQ
                  + jnp.arange(N_SEQ, dtype=jnp.int32)[:, None, None]) * PAGE
                 + jnp.arange(PAGE, dtype=jnp.int32)[None, None, :]).reshape(-1)
    causal = (jnp.arange(NEW, dtype=jnp.int32)[None, :] <= jnp.arange(NEW, dtype=jnp.int32)[:, None])[None, :, None, None, :]

    def decode_owner(inputs):
        owner, queries, table, request_len, pool_keys, pool_values, new_keys, new_values = inputs
        query_rows = queries.reshape(R_DEV, NEW, KVH, group_size, HD)
        owner_order = jnp.argsort((token_owner != owner).astype(jnp.int32), stable=True)[:capacity]
        received = token_owner[owner_order] == owner
        recv_keys = token_keys[owner_order].astype(jnp.float32)
        recv_values = token_values[owner_order].astype(jnp.float32)
        slots = table.reshape(R_DEV, N_SEQ, TBL)
        seq_ids = jnp.arange(N_SEQ, dtype=jnp.int32)[None, :, None]
        pools_k = pool_keys.reshape(POOL, N_SEQ, PAGE, KVH, HD).transpose(1, 0, 2, 3, 4).astype(jnp.float32)
        pools_v = pool_values.reshape(POOL, N_SEQ, PAGE, KVH, HD).transpose(1, 0, 2, 3, 4).astype(jnp.float32)
        cached_k = pools_k[seq_ids, slots].reshape(R_DEV, N_SEQ * TBL * PAGE, KVH, HD)
        cached_v = pools_v[seq_ids, slots].reshape(R_DEV, N_SEQ * TBL * PAGE, KVH, HD)
        cached_live = (positions[None, :] < request_len[:, None])[:, None, None, None, :]
        score_cache = jnp.einsum("rnkgd,rtkd->rnkgt", query_rows, cached_k, precision=highest) * scaling
        score_recv = jnp.einsum("rnkgd,tkd->rnkgt", query_rows, recv_keys, precision=highest) * scaling
        score_new = jnp.einsum("rnkgd,rjkd->rnkgj", query_rows, new_keys, precision=highest) * scaling
        row_peak = jnp.maximum(jnp.max(jnp.where(cached_live, score_cache, floor_score), axis=-1),
                               jnp.max(jnp.where(received, score_recv, floor_score), axis=-1))
        row_peak = jnp.maximum(row_peak, jnp.max(jnp.where(causal, score_new, floor_score), axis=-1))
        weight_cache = jnp.where(cached_live, jnp.exp(score_cache - row_peak[..., None]), 0.0)
        weight_recv = jnp.where(received, jnp.exp(score_recv - row_peak[..., None]), 0.0)
        weight_new = jnp.where(causal, jnp.exp(score_new - row_peak[..., None]), 0.0)
        row_total = jnp.sum(weight_cache, axis=-1) + jnp.sum(weight_recv, axis=-1) + jnp.sum(weight_new, axis=-1)
        mixture = jnp.einsum("rnkgt,rtkd->rnkgd", weight_cache, cached_v, precision=highest)
        mixture = mixture + jnp.einsum("rnkgt,tkd->rnkgd", weight_recv, recv_values, precision=highest)
        mixture = mixture + jnp.einsum("rnkgj,rjkd->rnkgd", weight_new, new_values, precision=highest)
        return (mixture / row_total[..., None]).reshape(R_DEV * NEW, QH * HD)

    attention = lax.map(decode_owner, (
        jnp.arange(N_BATCH, dtype=jnp.int32),
        dec_q.reshape(N_BATCH, R_DEV, NEW, QH * HD),
        tables.reshape(N_BATCH, R_DEV, N_SEQ * TBL),
        lengths.reshape(N_BATCH, R_DEV),
        cache_k.reshape(N_BATCH, POOL, N_SEQ * PAGE, KVH * HD),
        cache_v.reshape(N_BATCH, POOL, N_SEQ * PAGE, KVH * HD),
        dec_k.reshape(N_BATCH, R_DEV, NEW, KVH, HD),
        dec_v.reshape(N_BATCH, R_DEV, NEW, KVH, HD)))
    dec_out = jnp.dot(attention.reshape(REQS * NEW, QH * HD), w_out.astype(jnp.float32), precision=highest)
    return pre_out, dec_out.reshape(REQS, NEW, D)
```

```python
import jax
import jax.numpy as jnp
from jax import lax
from jax.experimental import pallas as pl
from jax.experimental.pallas import tpu as pltpu
from jax.sharding import PartitionSpec as P

HD = 128
PAGE = 16
NEW = 3
SLOTS = 2
FLOOR = -1e30
SCALE = HD ** (-0.5)
LOG2E = 1.4426950408889634
ABSENT = 1024.0
KEY_BLOCK = 256

f32 = jnp.float32
bf16 = jnp.bfloat16
MIB = 1024 * 1024
VMEM = pl.BlockSpec(memory_space=pltpu.VMEM)
SMEM = pl.BlockSpec(memory_space=pltpu.SMEM)
NT = (((1,), (1,)), ((), ()))


def dot(a, b, dims=(((1,), (0,)), ((), ()))):
    return lax.dot_general(a, b, dims, preferred_element_type=f32)


def split(x, terms):
    out = []
    for _ in range(terms):
        part = x.astype(bf16)
        out.append(part)
        x = x - part.astype(f32)
    return out


def pack_kernel(owner_ref, k_ref, v_ref, send_ref):
    cols = k_ref.shape[1]
    pages = k_ref.shape[0] // PAGE
    send_ref[:, :, :cols] = jnp.full((send_ref.shape[0], SLOTS * PAGE, cols), ABSENT, bf16)
    send_ref[:, :, cols:] = jnp.zeros((send_ref.shape[0], SLOTS * PAGE, cols), bf16)
    owners = [owner_ref[j] for j in range(pages)]
    for j in range(pages):
        slot = jnp.int32(0)
        for i in range(j):
            slot = slot + (owners[i] == owners[j]).astype(jnp.int32)
        slot = jnp.minimum(slot, SLOTS - 1)
        rows = pl.ds(pl.multiple_of(slot * PAGE, PAGE), PAGE)
        send_ref[owners[j], rows, :cols] = k_ref[j * PAGE : (j + 1) * PAGE, :]
        send_ref[owners[j], rows, cols:] = v_ref[j * PAGE : (j + 1) * PAGE, :]


def decode_kernel(
    seq_ref, table_ref, length_ref, q_ref, recv_ref, ck_ref, cv_ref, dk_ref, dv_ref,
    out_ref, q_wide, pool_k, pool_v,
):
    seq = seq_ref[0]
    heads = q_ref.shape[1] // HD
    half = heads // 2
    cols = ck_ref.shape[2]
    requests, entries = table_ref.shape
    lanes = heads * 8
    q_wide[...] = jnp.zeros_like(q_wide)
    for h in range(heads):
        at = (h // half) * HD
        q_wide[h * 8 : (h + 1) * 8, at : at + HD] = q_ref[:, h * HD : (h + 1) * HD]
    for r in range(requests):
        for j in range(entries):
            rows = slice((r * entries + j) * PAGE, (r * entries + j + 1) * PAGE)
            page = table_ref[r, j]
            pool_k[rows, :] = ck_ref[page]
            pool_v[rows, :] = cv_ref[page]
    queries = split(q_wide[...], 3)

    def scores_of(keys):
        total = dot(keys, queries[0], NT)
        for part in queries[1:]:
            total = total + dot(keys, part, NT)
        return total * SCALE

    recv_rows = recv_ref.shape[0]
    recv_k = recv_ref[:, :cols]
    recv_scores = scores_of(recv_k)
    recv_valid = jnp.broadcast_to(recv_k[:, 0:1].astype(f32) < 0.5 * ABSENT, (recv_rows, lanes))
    pool_rows = requests * entries * PAGE
    key_at = lax.broadcasted_iota(jnp.int32, (pool_rows, lanes), 0)
    lane = lax.broadcasted_iota(jnp.int32, (pool_rows, lanes), 1)
    lane_request = (lane % 8 >= NEW).astype(jnp.int32)
    key_request = key_at // (entries * PAGE)
    local_at = key_at % (entries * PAGE)
    position = ((local_at // PAGE) * 16 + seq) * PAGE + local_at % PAGE
    length = jnp.where(key_request == 0, length_ref[0], length_ref[1])
    pool_valid = (position < length) & (lane_request == key_request)
    pool_scores = scores_of(pool_k[...])
    new_at = lax.broadcasted_iota(jnp.int32, (8, lanes), 0)
    new_lane = lax.broadcasted_iota(jnp.int32, (8, lanes), 1) % 8
    new_lane_request = (new_lane >= NEW).astype(jnp.int32)
    new_request = (new_at >= NEW).astype(jnp.int32)
    new_valid = (
        (new_at < requests * NEW)
        & (new_request == new_lane_request)
        & (new_at - new_request * NEW <= new_lane - new_lane_request * NEW)
        & (seq == 0)
    )
    new_scores = (
        lax.dot_general(
            dk_ref[...], q_wide[...], NT, precision=lax.Precision.HIGHEST,
            preferred_element_type=f32,
        )
        * SCALE
    )
    parts = [(recv_scores, recv_valid), (pool_scores, pool_valid), (new_scores, new_valid)]
    peak = jnp.full((1, lanes), FLOOR, f32)
    for scores, valid in parts:
        masked = jnp.where(valid, scores, FLOOR)
        peak = jnp.maximum(peak, jnp.max(masked, axis=0, keepdims=True))
    weights = [jnp.where(valid, jnp.exp(scores - peak), 0.0) for scores, valid in parts]
    total = jnp.zeros((1, lanes), f32)
    for w in weights:
        total = total + jnp.sum(w, axis=0, keepdims=True)
    mixed = jnp.zeros((lanes, cols), f32)
    for w, values in ((weights[0], recv_ref[:, cols:]), (weights[1], pool_v[...])):
        for part in split(w.T, 2):
            mixed = mixed + dot(part, values)
    new_w = jnp.concatenate([weights[2], jnp.zeros((lanes - 8, lanes), f32)], axis=0).T
    new_v = jnp.concatenate([dv_ref[...], jnp.zeros((lanes - 8, cols), f32)], axis=0)
    mixed = mixed + lax.dot_general(
        new_w, new_v, (((1,), (0,)), ((), ())), precision=lax.Precision.HIGHEST,
        preferred_element_type=f32,
    )
    out_ref[: half * 8, :] = mixed[: half * 8, :HD]
    out_ref[half * 8 :, :] = mixed[half * 8 :, HD:]
    out_ref[6:7, :] = peak
    out_ref[7:8, :] = total


def finish_kernel(all_ref, w_ref, out_ref, attention):
    count = all_ref.shape[0]
    lanes = all_ref.shape[1]
    heads = lanes // 8
    peaks = jnp.concatenate([all_ref[s, 6:7, :] for s in range(count)], axis=0)
    totals = jnp.concatenate([all_ref[s, 7:8, :] for s in range(count)], axis=0)
    factor = jnp.exp(peaks - jnp.max(peaks, axis=0, keepdims=True))
    share = factor / jnp.sum(factor * totals, axis=0, keepdims=True)
    share = jnp.concatenate([share, jnp.zeros((lanes - count, lanes), f32)], axis=0).T
    mixed = share[:, 0:1] * all_ref[0]
    for s in range(1, count):
        mixed = mixed + share[:, s : s + 1] * all_ref[s]
    row = lax.broadcasted_iota(jnp.int32, (8, HD), 0)
    for h in range(heads):
        attention[:, h * HD : (h + 1) * HD] = jnp.where(row < 6, mixed[h * 8 : (h + 1) * 8, :], 0.0)
    w = w_ref[...]
    result = jnp.zeros(out_ref.shape, f32)
    for part in split(attention[...], 3):
        result = result + dot(part, w)
    out_ref[...] = result


def prefill_kernel(seq_ref, q_ref, kv_ref, out_ref, q_rows, scores, peaks, sums, mixed):
    seq = seq_ref[0]
    tokens = q_ref.shape[0]
    heads = q_ref.shape[1] // HD
    group = heads // 2
    rows = group * tokens
    last = seq * tokens // KEY_BLOCK
    lanes_of = KEY_BLOCK // HD

    def fold(x, op):
        out = x[:, :HD]
        for i in range(1, lanes_of):
            out = op(out, x[:, i * HD : (i + 1) * HD])
        return out

    for k in range(2):
        for a in range(group):
            h = k * group + a
            q_rows[a * tokens : (a + 1) * tokens, :] = q_ref[:, h * HD : (h + 1) * HD]
        peaks[...] = jnp.full(peaks.shape, FLOOR, f32)

        def score_block(j, masked):
            at = pl.multiple_of(j * KEY_BLOCK, KEY_BLOCK)
            s = dot(q_rows[...], kv_ref[pl.ds(at, KEY_BLOCK), k * HD : (k + 1) * HD], NT)
            if masked:
                q_at = lax.broadcasted_iota(jnp.int32, s.shape, 0) % tokens + seq * tokens
                k_at = lax.broadcasted_iota(jnp.int32, s.shape, 1) + at
                s = jnp.where(k_at <= q_at, s, FLOOR)
            scores[j] = s
            peaks[...] = jnp.maximum(peaks[...], fold(s, jnp.maximum))

        def first(j, carry):
            score_block(j, False)
            return carry

        lax.fori_loop(0, last, first, 0)
        score_block(last, True)
        peak = jnp.max(peaks[...], axis=1, keepdims=True)
        peaks[...] = jnp.broadcast_to(peak, peaks.shape)
        sums[...] = jnp.zeros_like(sums)
        mixed[...] = jnp.zeros_like(mixed)

        def second(j, carry):
            at = pl.multiple_of(j * KEY_BLOCK, KEY_BLOCK)
            p = jnp.exp2((scores[j] - jnp.concatenate([peaks[...]] * lanes_of, axis=1)) * (SCALE * LOG2E))
            sums[...] += fold(p, jnp.add)
            mixed[...] += dot(
                p.astype(bf16), kv_ref[pl.ds(at, KEY_BLOCK), (2 + k) * HD : (3 + k) * HD]
            )
            return carry

        lax.fori_loop(0, last + 1, second, 0)
        result = (mixed[...] / jnp.sum(sums[...], axis=1, keepdims=True)).astype(bf16)
        for a in range(group):
            h = k * group + a
            out_ref[:, h * HD : (h + 1) * HD] = result[a * tokens : (a + 1) * tokens, :]


def local(
    pre_q, pre_k, pre_v, owner_map, cache_k, cache_v, tables, lengths, dec_q, dec_k, dec_v, w_out
):
    seq = lax.axis_index("seq").astype(jnp.int32).reshape(1)
    owners = lax.axis_size("batch")
    tokens, cols = pre_k.shape[1], pre_k.shape[2]
    requests, new, q_cols = dec_q.shape
    lanes = q_cols // HD * 8

    kv = jnp.concatenate([pre_k[0], pre_v[0]], axis=1)
    all_kv = lax.all_gather(kv, "seq", axis=0, tiled=True)

    send = pl.pallas_call(
        pack_kernel,
        out_shape=jax.ShapeDtypeStruct((owners, SLOTS * PAGE, 2 * cols), bf16),
        in_specs=[SMEM, VMEM, VMEM],
        out_specs=VMEM,
        name="pack_pages",
    )(owner_map.reshape(-1), pre_k[0], pre_v[0])
    received = lax.all_to_all(send, "batch", 0, 0, tiled=True)

    def rows8(x):
        x = x.reshape(requests * new, x.shape[-1])
        return jnp.pad(x, ((0, 8 - requests * new), (0, 0)))

    partial_state = pl.pallas_call(
        decode_kernel,
        out_shape=jax.ShapeDtypeStruct((lanes, HD), f32),
        in_specs=[SMEM, SMEM, SMEM] + [VMEM] * 6,
        out_specs=VMEM,
        scratch_shapes=[
            pltpu.VMEM((lanes, 2 * HD), f32),
            pltpu.VMEM((requests * tables.shape[1] * PAGE, cols), bf16),
            pltpu.VMEM((requests * tables.shape[1] * PAGE, cols), bf16),
        ],
        compiler_params=pltpu.CompilerParams(vmem_limit_bytes=16 * MIB),
        name="decode_partial",
    )(
        seq, tables, lengths, rows8(dec_q),
        received.reshape(owners * SLOTS * PAGE, 2 * cols),
        cache_k, cache_v, rows8(dec_k), rows8(dec_v),
    )
    gathered = lax.all_gather(partial_state, "seq")
    projected = pl.pallas_call(
        finish_kernel,
        out_shape=jax.ShapeDtypeStruct((8, w_out.shape[1]), f32),
        in_specs=[VMEM, VMEM],
        out_specs=VMEM,
        scratch_shapes=[pltpu.VMEM((8, q_cols), f32)],
        compiler_params=pltpu.CompilerParams(vmem_limit_bytes=16 * MIB),
        name="finish_decode",
    )(gathered, w_out)
    mine = projected[: requests * new]
    other = lax.ppermute(mine, "tp", [(0, 1), (1, 0)])

    span = all_kv.shape[0]
    group = q_cols // HD // 2
    flops = 4 * 2 * group * tokens * span * HD
    pre_q, all_kv, mine = lax.optimization_barrier((pre_q, all_kv, mine))
    pre_out = pl.pallas_call(
        prefill_kernel,
        out_shape=jax.ShapeDtypeStruct((tokens, q_cols), bf16),
        in_specs=[SMEM, VMEM, VMEM],
        out_specs=VMEM,
        scratch_shapes=[
            pltpu.VMEM((group * tokens, HD), bf16),
            pltpu.VMEM((span // KEY_BLOCK, group * tokens, KEY_BLOCK), f32),
            pltpu.VMEM((group * tokens, HD), f32),
            pltpu.VMEM((group * tokens, HD), f32),
            pltpu.VMEM((group * tokens, HD), f32),
        ],
        compiler_params=pltpu.CompilerParams(vmem_limit_bytes=32 * MIB),
        cost_estimate=pl.CostEstimate(
            flops=flops, bytes_accessed=4 * MIB, transcendentals=2 * group * tokens * span
        ),
        name="prefill_attention",
    )(seq, pre_q[0], all_kv)
    dec_out = (mine + other).reshape(requests, new, w_out.shape[1])
    return (pre_out[None], dec_out)


def solution(mesh):
    placed = (
        P("batch", "seq", "tp"),
        P("batch", "seq", "tp"),
        P("batch", "seq", "tp"),
        P("batch", "seq", None),
        P("batch", "seq", "tp"),
        P("batch", "seq", "tp"),
        P("batch", "seq"),
        P("batch"),
        P("batch", None, "tp"),
        P("batch", None, "tp"),
        P("batch", None, "tp"),
        P("tp", "seq"),
    )
    return jax.shard_map(
        local,
        mesh=mesh,
        in_specs=placed,
        out_specs=(P("batch", "seq", "tp"), P("batch", None, "seq")),
        check_vma=False,
    )
```

```python
import jax
import jax.numpy as jnp
from jax import lax
from jax.experimental import pallas as pl
from jax.experimental.pallas import tpu as pltpu
from jax.sharding import PartitionSpec as P

HD = 128
PAGE = 16
NEW = 3
SLOTS = 2
FLOOR = -1e30
SCALE = HD ** (-0.5)
LOG2E = 1.4426950408889634
ABSENT = 1024.0
KEY_BLOCK = 256

f32 = jnp.float32
bf16 = jnp.bfloat16
MIB = 1024 * 1024
VMEM = pl.BlockSpec(memory_space=pltpu.VMEM)
SMEM = pl.BlockSpec(memory_space=pltpu.SMEM)
NT = (((1,), (1,)), ((), ()))


def dot(a, b, dims=(((1,), (0,)), ((), ()))):
    return lax.dot_general(a, b, dims, preferred_element_type=f32)


def split(x, terms):
    out = []
    for _ in range(terms):
        part = x.astype(bf16)
        out.append(part)
        x = x - part.astype(f32)
    return out


def pack_kernel(owner_ref, k_ref, v_ref, send_ref, kv_ref):
    cols = k_ref.shape[1]
    pages = k_ref.shape[0] // PAGE
    send_ref[:, :, :cols] = jnp.full((send_ref.shape[0], SLOTS * PAGE, cols), ABSENT, bf16)
    send_ref[:, :, cols:] = jnp.zeros((send_ref.shape[0], SLOTS * PAGE, cols), bf16)
    kv_ref[:, :cols] = k_ref[...]
    kv_ref[:, cols:] = v_ref[...]
    owners = [owner_ref[j] for j in range(pages)]
    for j in range(pages):
        slot = jnp.int32(0)
        for i in range(j):
            slot = slot + (owners[i] == owners[j]).astype(jnp.int32)
        slot = jnp.minimum(slot, SLOTS - 1)
        rows = pl.ds(pl.multiple_of(slot * PAGE, PAGE), PAGE)
        send_ref[owners[j], rows, :cols] = k_ref[j * PAGE : (j + 1) * PAGE, :]
        send_ref[owners[j], rows, cols:] = v_ref[j * PAGE : (j + 1) * PAGE, :]


def decode_kernel(
    seq_ref, table_ref, length_ref, q_ref, recv_ref, ck_ref, cv_ref, dk_ref, dv_ref,
    out_ref, q_wide, pool_k, pool_v,
):
    seq = seq_ref[0]
    heads = q_ref.shape[1] // HD
    half = heads // 2
    cols = ck_ref.shape[2]
    requests, entries = table_ref.shape
    each = requests * NEW
    rows_used = heads * each
    lanes = q_wide.shape[0]
    q_wide[...] = jnp.zeros_like(q_wide)
    for h in range(heads):
        at = (h // half) * HD
        q_wide[h * each : (h + 1) * each, at : at + HD] = q_ref[:each, h * HD : (h + 1) * HD]
    for r in range(requests):
        for j in range(entries):
            rows = slice((r * entries + j) * PAGE, (r * entries + j + 1) * PAGE)
            page = table_ref[r, j]
            pool_k[rows, :] = ck_ref[page]
            pool_v[rows, :] = cv_ref[page]
    queries = split(q_wide[...], 3)

    def scores_of(keys):
        total = dot(keys, queries[0], NT)
        for part in queries[1:]:
            total = total + dot(keys, part, NT)
        return total * SCALE

    recv_rows = recv_ref.shape[0]
    recv_k = recv_ref[:, :cols]
    recv_scores = scores_of(recv_k)
    recv_valid = jnp.broadcast_to(recv_k[:, 0:1].astype(f32) < 0.5 * ABSENT, (recv_rows, lanes))
    pool_rows = requests * entries * PAGE
    key_at = lax.broadcasted_iota(jnp.int32, (pool_rows, lanes), 0)
    lane = lax.broadcasted_iota(jnp.int32, (pool_rows, lanes), 1)
    lane_request = (lane % each >= NEW).astype(jnp.int32)
    key_request = key_at // (entries * PAGE)
    local_at = key_at % (entries * PAGE)
    position = ((local_at // PAGE) * 16 + seq) * PAGE + local_at % PAGE
    length = jnp.where(key_request == 0, length_ref[0], length_ref[1])
    pool_valid = (position < length) & (lane_request == key_request)
    pool_scores = scores_of(pool_k[...])
    new_at = lax.broadcasted_iota(jnp.int32, (8, lanes), 0)
    new_lane = lax.broadcasted_iota(jnp.int32, (8, lanes), 1) % each
    new_lane_request = (new_lane >= NEW).astype(jnp.int32)
    new_request = (new_at >= NEW).astype(jnp.int32)
    new_valid = (
        (new_at < each)
        & (new_request == new_lane_request)
        & (new_at - new_request * NEW <= new_lane - new_lane_request * NEW)
        & (seq == 0)
    )
    new_scores = (
        lax.dot_general(
            dk_ref[...], q_wide[...], NT, precision=lax.Precision.HIGHEST,
            preferred_element_type=f32,
        )
        * SCALE
    )
    parts = [(recv_scores, recv_valid), (pool_scores, pool_valid), (new_scores, new_valid)]
    peak = jnp.full((1, lanes), FLOOR, f32)
    for scores, valid in parts:
        masked = jnp.where(valid, scores, FLOOR)
        peak = jnp.maximum(peak, jnp.max(masked, axis=0, keepdims=True))
    weights = [jnp.where(valid, jnp.exp(scores - peak), 0.0) for scores, valid in parts]
    total = jnp.zeros((1, lanes), f32)
    for w in weights:
        total = total + jnp.sum(w, axis=0, keepdims=True)
    mixed = jnp.zeros((lanes, cols), f32)
    for w, values in ((weights[0], recv_ref[:, cols:]), (weights[1], pool_v[...])):
        for part in split(w.T, 2):
            mixed = mixed + dot(part, values)
    new_w = jnp.concatenate([weights[2], jnp.zeros((lanes - 8, lanes), f32)], axis=0).T
    new_v = jnp.concatenate([dv_ref[...], jnp.zeros((lanes - 8, cols), f32)], axis=0)
    mixed = mixed + lax.dot_general(
        new_w, new_v, (((1,), (0,)), ((), ())), precision=lax.Precision.HIGHEST,
        preferred_element_type=f32,
    )
    out_ref[: half * each, :] = mixed[: half * each, :HD]
    out_ref[half * each : rows_used, :] = mixed[half * each : rows_used, HD:]
    out_ref[rows_used : rows_used + 1, :] = peak
    out_ref[rows_used + 1 : rows_used + 2, :] = total
    out_ref[rows_used + 2 :, :] = jnp.zeros((out_ref.shape[0] - rows_used - 2, HD), f32)


def finish_kernel(all_ref, w_ref, out_ref, attention):
    count = all_ref.shape[0]
    heads = attention.shape[1] // HD
    rows_used = all_ref.shape[1] - 8
    each = rows_used // heads
    peaks = jnp.concatenate([all_ref[s, rows_used : rows_used + 1, :] for s in range(count)], axis=0)
    totals = jnp.concatenate(
        [all_ref[s, rows_used + 1 : rows_used + 2, :] for s in range(count)], axis=0
    )
    factor = jnp.exp(peaks - jnp.max(peaks, axis=0, keepdims=True))
    share = factor / jnp.sum(factor * totals, axis=0, keepdims=True)
    share = jnp.concatenate([share, jnp.zeros((HD - count, HD), f32)], axis=0).T[:rows_used]
    mixed = share[:, 0:1] * all_ref[0, :rows_used, :]
    for s in range(1, count):
        mixed = mixed + share[:, s : s + 1] * all_ref[s, :rows_used, :]
    attention[...] = jnp.zeros_like(attention)
    for h in range(heads):
        attention[:each, h * HD : (h + 1) * HD] = mixed[h * each : (h + 1) * each, :]
    w = w_ref[...]
    result = jnp.zeros(out_ref.shape, f32)
    for part in split(attention[...], 3):
        result = result + dot(part, w)
    out_ref[...] = result


def prefill_kernel(seq_ref, q_ref, kv_ref, out_ref, q_rows, scores, peaks, sums, mixed):
    seq = seq_ref[0]
    tokens = q_ref.shape[0]
    heads = q_ref.shape[1] // HD
    group = heads // 2
    rows = group * tokens
    last = seq * tokens // KEY_BLOCK
    lanes_of = KEY_BLOCK // HD

    def fold(x, op):
        out = x[:, :HD]
        for i in range(1, lanes_of):
            out = op(out, x[:, i * HD : (i + 1) * HD])
        return out

    for k in range(2):
        for a in range(group):
            h = k * group + a
            q_rows[a * tokens : (a + 1) * tokens, :] = q_ref[:, h * HD : (h + 1) * HD]
        peaks[...] = jnp.full(peaks.shape, FLOOR, f32)

        def score_block(j, masked):
            at = pl.multiple_of(j * KEY_BLOCK, KEY_BLOCK)
            s = dot(q_rows[...], kv_ref[pl.ds(at, KEY_BLOCK), k * HD : (k + 1) * HD], NT)
            if masked:
                q_at = lax.broadcasted_iota(jnp.int32, s.shape, 0) % tokens + seq * tokens
                k_at = lax.broadcasted_iota(jnp.int32, s.shape, 1) + at
                s = jnp.where(k_at <= q_at, s, FLOOR)
            scores[j] = s
            peaks[...] = jnp.maximum(peaks[...], fold(s, jnp.maximum))

        def first(j, carry):
            score_block(j, False)
            return carry

        lax.fori_loop(0, last, first, 0)
        score_block(last, True)
        peak = jnp.max(peaks[...], axis=1, keepdims=True)
        peaks[...] = jnp.broadcast_to(peak, peaks.shape)
        sums[...] = jnp.zeros_like(sums)
        mixed[...] = jnp.zeros_like(mixed)

        def second(j, carry):
            at = pl.multiple_of(j * KEY_BLOCK, KEY_BLOCK)
            p = jnp.exp2((scores[j] - jnp.concatenate([peaks[...]] * lanes_of, axis=1)) * (SCALE * LOG2E))
            sums[...] += fold(p, jnp.add)
            mixed[...] += dot(
                p.astype(bf16), kv_ref[pl.ds(at, KEY_BLOCK), (2 + k) * HD : (3 + k) * HD]
            )
            return carry

        lax.fori_loop(0, last + 1, second, 0)
        result = (mixed[...] / jnp.sum(sums[...], axis=1, keepdims=True)).astype(bf16)
        for a in range(group):
            h = k * group + a
            out_ref[:, h * HD : (h + 1) * HD] = result[a * tokens : (a + 1) * tokens, :]


def local(
    pre_q, pre_k, pre_v, owner_map, cache_k, cache_v, tables, lengths, dec_q, dec_k, dec_v, w_out
):
    seq = lax.axis_index("seq").astype(jnp.int32).reshape(1)
    owners = lax.axis_size("batch")
    tokens, cols = pre_k.shape[1], pre_k.shape[2]
    requests, new, q_cols = dec_q.shape
    rows_used = q_cols // HD * requests * new

    send, kv = pl.pallas_call(
        pack_kernel,
        out_shape=(
            jax.ShapeDtypeStruct((owners, SLOTS * PAGE, 2 * cols), bf16),
            jax.ShapeDtypeStruct((tokens, 2 * cols), bf16),
        ),
        in_specs=[SMEM, VMEM, VMEM],
        out_specs=(VMEM, VMEM),
        name="pack_pages",
    )(owner_map.reshape(-1), pre_k[0], pre_v[0])
    all_kv = lax.all_gather(kv, "seq", axis=0, tiled=True)
    received = lax.all_to_all(send, "batch", 0, 0, tiled=True)

    def rows8(x):
        x = x.reshape(requests * new, x.shape[-1])
        return jnp.pad(x, ((0, 8 - requests * new), (0, 0)))

    partial_state = pl.pallas_call(
        decode_kernel,
        out_shape=jax.ShapeDtypeStruct((rows_used + 8, HD), f32),
        in_specs=[SMEM, SMEM, SMEM] + [VMEM] * 6,
        out_specs=VMEM,
        scratch_shapes=[
            pltpu.VMEM((HD, 2 * HD), f32),
            pltpu.VMEM((requests * tables.shape[1] * PAGE, cols), bf16),
            pltpu.VMEM((requests * tables.shape[1] * PAGE, cols), bf16),
        ],
        compiler_params=pltpu.CompilerParams(vmem_limit_bytes=16 * MIB),
        name="decode_partial",
    )(
        seq, tables, lengths, rows8(dec_q),
        received.reshape(owners * SLOTS * PAGE, 2 * cols),
        cache_k, cache_v, rows8(dec_k), rows8(dec_v),
    )
    gathered = lax.all_gather(partial_state, "seq")
    gathered, all_kv = lax.optimization_barrier((gathered, all_kv))
    projected = pl.pallas_call(
        finish_kernel,
        out_shape=jax.ShapeDtypeStruct((8, w_out.shape[1]), f32),
        in_specs=[VMEM, VMEM],
        out_specs=VMEM,
        scratch_shapes=[pltpu.VMEM((8, q_cols), f32)],
        compiler_params=pltpu.CompilerParams(vmem_limit_bytes=16 * MIB),
        name="finish_decode",
    )(gathered, w_out)
    mine = projected[: requests * new]
    other = lax.ppermute(mine, "tp", [(0, 1), (1, 0)])

    span = all_kv.shape[0]
    group = q_cols // HD // 2
    flops = 4 * 2 * group * tokens * span * HD
    pre_q, all_kv, mine = lax.optimization_barrier((pre_q, all_kv, mine))
    pre_out = pl.pallas_call(
        prefill_kernel,
        out_shape=jax.ShapeDtypeStruct((tokens, q_cols), bf16),
        in_specs=[SMEM, VMEM, VMEM],
        out_specs=VMEM,
        scratch_shapes=[
            pltpu.VMEM((group * tokens, HD), bf16),
            pltpu.VMEM((span // KEY_BLOCK, group * tokens, KEY_BLOCK), f32),
            pltpu.VMEM((group * tokens, HD), f32),
            pltpu.VMEM((group * tokens, HD), f32),
            pltpu.VMEM((group * tokens, HD), f32),
        ],
        compiler_params=pltpu.CompilerParams(vmem_limit_bytes=32 * MIB),
        cost_estimate=pl.CostEstimate(
            flops=flops, bytes_accessed=4 * MIB, transcendentals=2 * group * tokens * span
        ),
        name="prefill_attention",
    )(seq, pre_q[0], all_kv)
    dec_out = (mine + other).reshape(requests, new, w_out.shape[1])
    return (pre_out[None], dec_out)


def solution(mesh):
    placed = (
        P("batch", "seq", "tp"),
        P("batch", "seq", "tp"),
        P("batch", "seq", "tp"),
        P("batch", "seq", None),
        P("batch", "seq", "tp"),
        P("batch", "seq", "tp"),
        P("batch", "seq"),
        P("batch"),
        P("batch", None, "tp"),
        P("batch", None, "tp"),
        P("batch", None, "tp"),
        P("tp", "seq"),
    )
    return jax.shard_map(
        local,
        mesh=mesh,
        in_specs=placed,
        out_specs=(P("batch", "seq", "tp"), P("batch", None, "seq")),
        check_vma=False,
    )
```

```python
import jax
import jax.numpy as jnp
from jax import lax
from jax.experimental import pallas as pl
from jax.experimental.pallas import tpu as pltpu
from jax.sharding import Mesh
from jax.sharding import PartitionSpec as P

HD = 128
PAGE = 16
NEW = 3
SLOTS = 2
CHUNK = 512
FLOOR = -1e30
SCALE = HD ** (-0.5)
LOG2E = 1.4426950408889634
ABSENT = 1024.0

SEQ = ("z", "core")
BATCH = ("y", "x")

f32 = jnp.float32
bf16 = jnp.bfloat16
MIB = 1024 * 1024
VMEM = pl.BlockSpec(memory_space=pltpu.VMEM)
SMEM = pl.BlockSpec(memory_space=pltpu.SMEM)
ANY = pl.BlockSpec(memory_space=pl.ANY)
NT = (((1,), (1,)), ((), ()))
NN = (((1,), (0,)), ((), ()))


def dot(a, b, dims=NN):
    return lax.dot_general(a, b, dims, preferred_element_type=f32)


def exact_dot(a, b, dims=NN):
    return lax.dot_general(
        a, b, dims, precision=lax.Precision.HIGHEST, preferred_element_type=f32
    )


def split(x, terms):
    out = []
    for _ in range(terms):
        part = x.astype(bf16)
        out.append(part)
        x = x - part.astype(f32)
    return out


def down(row, count):
    return jnp.broadcast_to(row, (row.shape[1], row.shape[1])).T[:count]


def pack_kernel(owner_ref, k_ref, v_ref, send_ref, kv_ref):
    cols = k_ref.shape[1]
    pages = k_ref.shape[0] // PAGE
    send_ref[:, :, :cols] = jnp.full((send_ref.shape[0], SLOTS * PAGE, cols), ABSENT, bf16)
    send_ref[:, :, cols:] = jnp.zeros((send_ref.shape[0], SLOTS * PAGE, cols), bf16)
    kv_ref[:, :cols] = k_ref[...]
    kv_ref[:, cols:] = v_ref[...]
    owners = [owner_ref[j] for j in range(pages)]
    for j in range(pages):
        slot = jnp.int32(0)
        for i in range(j):
            slot = slot + (owners[i] == owners[j]).astype(jnp.int32)
        slot = jnp.minimum(slot, SLOTS - 1)
        rows = pl.ds(pl.multiple_of(slot * PAGE, PAGE), PAGE)
        send_ref[owners[j], rows, :cols] = k_ref[j * PAGE : (j + 1) * PAGE, :]
        send_ref[owners[j], rows, cols:] = v_ref[j * PAGE : (j + 1) * PAGE, :]


def cached_kernel(
    seq_ref, table_ref, length_ref, q_ref, ck_ref, cv_ref, dk_ref, dv_ref,
    terms_ref, state_ref, mixed_ref, q_wide, pool_k, pool_v,
):
    seq = seq_ref[0]
    heads = q_ref.shape[1] // HD
    half = heads // 2
    requests, entries = table_ref.shape
    each = requests * NEW
    rows_used = heads * each
    lanes = q_wide.shape[0]
    cols = ck_ref.shape[2]
    q_wide[...] = jnp.zeros_like(q_wide)
    for h in range(heads):
        at = (h // half) * HD
        q_wide[h * each : (h + 1) * each, at : at + HD] = q_ref[:each, h * HD : (h + 1) * HD]
    for r in range(requests):
        for j in range(entries):
            rows = slice((r * entries + j) * PAGE, (r * entries + j + 1) * PAGE)
            page = table_ref[r, j]
            pool_k[rows, :] = ck_ref[page]
            pool_v[rows, :] = cv_ref[page]
    terms = split(q_wide[...], 3)
    for i, part in enumerate(terms):
        terms_ref[i] = part
    pool_scores = sum(dot(pool_k[...], part, NT) for part in terms) * SCALE
    pool_rows = requests * entries * PAGE
    key_at = lax.broadcasted_iota(jnp.int32, (pool_rows, lanes), 0)
    lane = lax.broadcasted_iota(jnp.int32, (pool_rows, lanes), 1)
    lane_request = lane % requests
    key_request = key_at // (entries * PAGE)
    local_at = key_at % (entries * PAGE)
    position = ((local_at // PAGE) * 16 + seq) * PAGE + local_at % PAGE
    length = jnp.where(key_request == 0, length_ref[0], length_ref[1])
    pool_valid = (position < length) & (lane_request == key_request)
    new_at = lax.broadcasted_iota(jnp.int32, (8, lanes), 0)
    new_lane = lax.broadcasted_iota(jnp.int32, (8, lanes), 1) % each
    new_valid = (
        (new_at < each)
        & (new_at % requests == new_lane % requests)
        & (new_at // requests <= new_lane // requests)
        & (seq == 0)
    )
    new_scores = exact_dot(dk_ref[...], q_wide[...], NT) * SCALE
    peak = jnp.maximum(
        jnp.max(jnp.where(pool_valid, pool_scores, FLOOR), axis=0, keepdims=True),
        jnp.max(jnp.where(new_valid, new_scores, FLOOR), axis=0, keepdims=True),
    )
    pool_w = jnp.where(pool_valid, jnp.exp(pool_scores - peak), 0.0)
    new_w = jnp.where(new_valid, jnp.exp(new_scores - peak), 0.0)
    total = jnp.sum(pool_w, axis=0, keepdims=True) + jnp.sum(new_w, axis=0, keepdims=True)
    mixed = sum(dot(part, pool_v[...]) for part in split(pool_w.T, 3))
    tall_w = jnp.concatenate([new_w, jnp.zeros((lanes - 8, lanes), f32)], axis=0).T
    tall_v = jnp.concatenate([dv_ref[...], jnp.zeros((lanes - 8, cols), f32)], axis=0)
    mixed = mixed + exact_dot(tall_w, tall_v)
    mixed_ref[: half * each, :] = mixed[: half * each, :HD]
    mixed_ref[half * each : rows_used, :] = mixed[half * each : rows_used, HD:]
    state_ref[0:1, :] = peak
    state_ref[1:2, :] = total
    state_ref[2:, :] = jnp.zeros((6, lanes), f32)


def received_kernel(terms_ref, state_ref, mixed_ref, recv_ref, out_ref):
    lanes = terms_ref.shape[1]
    cols = terms_ref.shape[2]
    rows_used = mixed_ref.shape[0]
    half = rows_used // 2
    recv_rows = recv_ref.shape[0]
    keys = recv_ref[:, :cols]
    scores = sum(dot(keys, terms_ref[i], NT) for i in range(3)) * SCALE
    valid = jnp.broadcast_to(keys[:, 0:1].astype(f32) < 0.5 * ABSENT, (recv_rows, lanes))
    before = state_ref[0:1, :]
    peak = jnp.maximum(
        before, jnp.max(jnp.where(valid, scores, FLOOR), axis=0, keepdims=True)
    )
    weights = jnp.where(valid, jnp.exp(scores - peak), 0.0)
    factor = jnp.exp(before - peak)
    total = state_ref[1:2, :] * factor + jnp.sum(weights, axis=0, keepdims=True)
    mixed = sum(dot(part, recv_ref[:, cols:]) for part in split(weights.T, 3))
    kept = mixed_ref[...] * down(factor, rows_used)
    out_ref[:half, :] = kept[:half] + mixed[:half, :HD]
    out_ref[half:rows_used, :] = kept[half:] + mixed[half:rows_used, HD:]
    out_ref[rows_used : rows_used + 1, :] = peak
    out_ref[rows_used + 1 : rows_used + 2, :] = total
    out_ref[rows_used + 2 :, :] = jnp.zeros((6, lanes), f32)


def finish_kernel(all_ref, w_ref, out_ref, attention):
    count = all_ref.shape[0]
    heads = attention.shape[1] // HD
    rows_used = all_ref.shape[1] - 8
    each = rows_used // heads
    peaks = jnp.concatenate([all_ref[s, rows_used : rows_used + 1, :] for s in range(count)], axis=0)
    totals = jnp.concatenate(
        [all_ref[s, rows_used + 1 : rows_used + 2, :] for s in range(count)], axis=0
    )
    factor = jnp.exp(peaks - jnp.max(peaks, axis=0, keepdims=True))
    share = factor / jnp.sum(factor * totals, axis=0, keepdims=True)
    share = jnp.concatenate([share, jnp.zeros((HD - count, HD), f32)], axis=0).T[:rows_used]
    mixed = share[:, 0:1] * all_ref[0, :rows_used, :]
    for s in range(1, count):
        mixed = mixed + share[:, s : s + 1] * all_ref[s, :rows_used, :]
    attention[...] = jnp.zeros_like(attention)
    for h in range(heads):
        attention[:each, h * HD : (h + 1) * HD] = mixed[h * each : (h + 1) * each, :]
    w = w_ref[...]
    result = jnp.zeros((8, w.shape[1]), f32)
    for part in split(attention[...], 3):
        result = result + dot(part, w)
    pair = out_ref.shape[1]
    for n in range(out_ref.shape[0]):
        out_ref[n] = result[n * pair : (n + 1) * pair, :]


def prefill_kernel(seq_ref, q_hbm, kv_hbm, out_ref, q_ref, kv_ref, sems):
    seq = seq_ref[0]
    tokens = q_ref.shape[0]
    heads = q_ref.shape[1] // HD
    span = kv_ref.shape[0]
    group = heads // 2
    columns = [slice(i * HD, (i + 1) * HD) for i in range(4)]
    def attend(low, width):
        chunk = min(CHUNK, width - low)
        copies = [
            pltpu.make_async_copy(q_hbm, q_ref, sems.at[0]),
            pltpu.make_async_copy(kv_hbm.at[:width], kv_ref.at[:width], sems.at[1]),
        ]
        for copy in copies:
            copy.start()
        for copy in copies:
            copy.wait()
        q_at = lax.broadcasted_iota(jnp.int32, (2 * tokens, width - low), 0) % tokens + seq * tokens
        k_at = lax.broadcasted_iota(jnp.int32, (2 * tokens, width - low), 1) + low
        visible = k_at <= q_at

        def scores_of(pair):
            k = 2 * pair // group
            q = jnp.concatenate(
                [q_ref[:, h * HD : (h + 1) * HD] for h in (2 * pair, 2 * pair + 1)], axis=0
            )
            blocks = []
            for c in range(0, width, chunk):
                s = dot(q, kv_ref[c : c + chunk, columns[k]], NT)
                if c >= low:
                    s = jnp.where(visible[:, c - low : c - low + chunk], s, FLOOR)
                blocks.append(s)
            return blocks

        def finish(pair, blocks):
            k = 2 * pair // group
            peak = blocks[0]
            for s in blocks[1:]:
                peak = jnp.maximum(peak, s)
            peak = jnp.max(peak, axis=1, keepdims=True)
            mixed, total = None, None
            for i, s in enumerate(blocks):
                p = jnp.exp2((s - peak) * (SCALE * LOG2E))
                part = dot(p.astype(bf16), kv_ref[i * chunk : (i + 1) * chunk, columns[2 + k]])
                mixed = part if mixed is None else mixed + part
                total = p if total is None else total + p
            result = (mixed / jnp.sum(total, axis=1, keepdims=True)).astype(bf16)
            for n, h in enumerate((2 * pair, 2 * pair + 1)):
                out_ref[:, h * HD : (h + 1) * HD] = result[n * tokens : (n + 1) * tokens, :]

        now = scores_of(0)
        for pair in range(heads // 2):
            later = scores_of(pair + 1) if pair + 1 < heads // 2 else None
            finish(pair, now)
            now = later

    low, width = 0, 2 * tokens
    while low < span:
        inside = (seq * tokens >= low) & (seq * tokens < width)
        pl.when(inside)(lambda low=low, width=width: attend(low, width))
        low, width = width, 2 * width


def local(
    pre_q, pre_k, pre_v, owner_map, cache_k, cache_v, tables, lengths, dec_q, dec_k, dec_v, w_out
):
    seq = lax.axis_index(SEQ).astype(jnp.int32).reshape(1)
    owners = lax.axis_size(BATCH)
    swap = [(0, 1), (1, 0)]
    tokens, cols = pre_k.shape[1], pre_k.shape[2]
    requests, new, q_cols = dec_q.shape
    rows_used = q_cols // HD * requests * new
    small = pltpu.CompilerParams(vmem_limit_bytes=16 * MIB)

    def rows8(x):
        x = x.transpose(1, 0, 2).reshape(requests * new, x.shape[-1])
        return jnp.pad(x, ((0, 8 - requests * new), (0, 0)))

    send, kv = pl.pallas_call(
        pack_kernel,
        out_shape=(
            jax.ShapeDtypeStruct((owners, SLOTS * PAGE, 2 * cols), bf16),
            jax.ShapeDtypeStruct((tokens, 2 * cols), bf16),
        ),
        in_specs=[SMEM, VMEM, VMEM],
        out_specs=(VMEM, VMEM),
        name="pack_pages",
    )(owner_map.reshape(-1), pre_k[0], pre_v[0])
    received = lax.all_to_all(send, BATCH, 0, 0, tiled=True)

    all_kv = lax.all_gather(kv, SEQ, axis=0, tiled=True)
    entries = tables.shape[1]
    terms, state, mixed = pl.pallas_call(
        cached_kernel,
        out_shape=(
            jax.ShapeDtypeStruct((3, HD, 2 * HD), bf16),
            jax.ShapeDtypeStruct((8, HD), f32),
            jax.ShapeDtypeStruct((rows_used, HD), f32),
        ),
        in_specs=[SMEM, SMEM, SMEM] + [VMEM] * 5,
        out_specs=(VMEM, VMEM, VMEM),
        scratch_shapes=[
            pltpu.VMEM((HD, 2 * HD), f32),
            pltpu.VMEM((requests * entries * PAGE, cols), bf16),
            pltpu.VMEM((requests * entries * PAGE, cols), bf16),
        ],
        compiler_params=small,
        name="cached_partial",
    )(
        seq, tables, lengths, rows8(dec_q), cache_k, cache_v,
        rows8(dec_k), rows8(dec_v),
    )
    partial_state = pl.pallas_call(
        received_kernel,
        out_shape=jax.ShapeDtypeStruct((rows_used + 8, HD), f32),
        in_specs=[VMEM] * 4,
        out_specs=VMEM,
        compiler_params=small,
        name="received_partial",
    )(terms, state, mixed, received.reshape(owners * SLOTS * PAGE, 2 * cols))
    gathered = lax.all_gather(partial_state, SEQ)
    mine = pl.pallas_call(
        finish_kernel,
        out_shape=jax.ShapeDtypeStruct((new, requests, w_out.shape[1]), f32),
        in_specs=[VMEM, VMEM],
        out_specs=VMEM,
        scratch_shapes=[pltpu.VMEM((8, q_cols), f32)],
        compiler_params=small,
        name="finish_decode",
    )(gathered, w_out)
    other = lax.ppermute(mine, "tp", swap)

    group = q_cols // HD // 2
    span = all_kv.shape[0]
    pre_q, all_kv, mine = lax.optimization_barrier((pre_q, all_kv, mine))
    pre_out = pl.pallas_call(
        prefill_kernel,
        out_shape=jax.ShapeDtypeStruct((tokens, q_cols), bf16),
        in_specs=[SMEM, ANY, ANY],
        out_specs=VMEM,
        scratch_shapes=[
            pltpu.VMEM((tokens, q_cols), bf16),
            pltpu.VMEM((span, 2 * cols), bf16),
            pltpu.SemaphoreType.DMA((2,)),
        ],
        compiler_params=pltpu.CompilerParams(vmem_limit_bytes=60 * MIB),
        cost_estimate=pl.CostEstimate(
            flops=8 * group * tokens * span * HD,
            bytes_accessed=4 * MIB,
            transcendentals=2 * group * tokens * span,
        ),
        name="prefill_attention",
    )(seq, pre_q[0], all_kv)
    pre_out, other = lax.optimization_barrier((pre_out, other))
    dec_out = (mine + other).transpose(1, 0, 2)
    return (pre_out[None], dec_out)


def solution(mesh):
    cut = Mesh(mesh.devices.reshape(8, 2, 4, 4, 2), ("z", "core", "y", "x", "tp"))
    placed = (
        P(BATCH, SEQ, "tp"),
        P(BATCH, SEQ, "tp"),
        P(BATCH, SEQ, "tp"),
        P(BATCH, SEQ, None),
        P(BATCH, SEQ, "tp"),
        P(BATCH, SEQ, "tp"),
        P(BATCH, SEQ),
        P(BATCH),
        P(BATCH, None, "tp"),
        P(BATCH, None, "tp"),
        P(BATCH, None, "tp"),
        P("tp", SEQ),
    )
    return jax.shard_map(
        local,
        mesh=cut,
        in_specs=placed,
        out_specs=(P(BATCH, SEQ, "tp"), P(BATCH, None, SEQ)),
        check_vma=False,
    )
```

```python
import jax
import jax.numpy as jnp
from jax import lax
from jax.experimental import pallas as pl
from jax.experimental.pallas import tpu as pltpu
from jax.sharding import Mesh
from jax.sharding import PartitionSpec as P

HD = 128
PAGE = 16
NEW = 3
SLOTS = 2
CHUNK = 512
TAIL = 16
FLOOR = -1e30
SCALE = HD ** (-0.5)
LOG2E = 1.4426950408889634
ABSENT = 1024.0

SEQ = ("z", "core")
BATCH = ("y", "x")

f32 = jnp.float32
bf16 = jnp.bfloat16
MIB = 1024 * 1024
VMEM = pl.BlockSpec(memory_space=pltpu.VMEM)
SMEM = pl.BlockSpec(memory_space=pltpu.SMEM)
ANY = pl.BlockSpec(memory_space=pl.ANY)
NT = (((1,), (1,)), ((), ()))
NN = (((1,), (0,)), ((), ()))


def dot(a, b, dims=NN):
    return lax.dot_general(a, b, dims, preferred_element_type=f32)


def exact_dot(a, b, dims=NN):
    return lax.dot_general(
        a, b, dims, precision=lax.Precision.HIGHEST, preferred_element_type=f32
    )


def split(x, terms):
    out = []
    for _ in range(terms):
        part = x.astype(bf16)
        out.append(part)
        x = x - part.astype(f32)
    return out


def down(row, count):
    return jnp.broadcast_to(row, (row.shape[1], row.shape[1])).T[:count]


def pack_kernel(owner_ref, k_ref, v_ref, send_ref, kv_ref):
    cols = k_ref.shape[1]
    pages = k_ref.shape[0] // PAGE
    send_ref[:, :, :cols] = jnp.full((send_ref.shape[0], SLOTS * PAGE, cols), ABSENT, bf16)
    send_ref[:, :, cols:] = jnp.zeros((send_ref.shape[0], SLOTS * PAGE, cols), bf16)
    kv_ref[:, :cols] = k_ref[...]
    kv_ref[:, cols:] = v_ref[...]
    owners = [owner_ref[j] for j in range(pages)]
    for j in range(pages):
        slot = jnp.int32(0)
        for i in range(j):
            slot = slot + (owners[i] == owners[j]).astype(jnp.int32)
        slot = jnp.minimum(slot, SLOTS - 1)
        rows = pl.ds(pl.multiple_of(slot * PAGE, PAGE), PAGE)
        send_ref[owners[j], rows, :cols] = k_ref[j * PAGE : (j + 1) * PAGE, :]
        send_ref[owners[j], rows, cols:] = v_ref[j * PAGE : (j + 1) * PAGE, :]


def cached_kernel(
    seq_ref, table_ref, length_ref, q_ref, ck_ref, cv_ref, dk_ref, dv_ref,
    terms_ref, state_ref, mixed_ref, q_wide, pool_k, pool_v,
):
    seq = seq_ref[0]
    heads = q_ref.shape[1] // HD
    half = heads // 2
    requests, entries = table_ref.shape
    each = requests * NEW
    rows_used = heads * each
    lanes = q_wide.shape[0]
    cols = ck_ref.shape[2]
    q_wide[...] = jnp.zeros_like(q_wide)
    for h in range(heads):
        at = (h // half) * HD
        q_wide[h * each : (h + 1) * each, at : at + HD] = q_ref[:each, h * HD : (h + 1) * HD]
    for r in range(requests):
        for j in range(entries):
            rows = slice((r * entries + j) * PAGE, (r * entries + j + 1) * PAGE)
            page = table_ref[r, j]
            pool_k[rows, :] = ck_ref[page]
            pool_v[rows, :] = cv_ref[page]
    terms = split(q_wide[...], 3)
    for i, part in enumerate(terms):
        terms_ref[i] = part
    pool_scores = sum(dot(pool_k[...], part, NT) for part in terms) * SCALE
    pool_rows = requests * entries * PAGE
    key_at = lax.broadcasted_iota(jnp.int32, (pool_rows, lanes), 0)
    lane = lax.broadcasted_iota(jnp.int32, (pool_rows, lanes), 1)
    lane_request = lane % requests
    key_request = key_at // (entries * PAGE)
    local_at = key_at % (entries * PAGE)
    position = ((local_at // PAGE) * 16 + seq) * PAGE + local_at % PAGE
    length = jnp.where(key_request == 0, length_ref[0], length_ref[1])
    pool_valid = (position < length) & (lane_request == key_request)
    new_at = lax.broadcasted_iota(jnp.int32, (8, lanes), 0)
    new_lane = lax.broadcasted_iota(jnp.int32, (8, lanes), 1) % each
    new_valid = (
        (new_at < each)
        & (new_at % requests == new_lane % requests)
        & (new_at // requests <= new_lane // requests)
        & (seq == 0)
    )
    new_scores = exact_dot(dk_ref[...], q_wide[...], NT) * SCALE
    peak = jnp.maximum(
        jnp.max(jnp.where(pool_valid, pool_scores, FLOOR), axis=0, keepdims=True),
        jnp.max(jnp.where(new_valid, new_scores, FLOOR), axis=0, keepdims=True),
    )
    pool_w = jnp.where(pool_valid, jnp.exp(pool_scores - peak), 0.0)
    new_w = jnp.where(new_valid, jnp.exp(new_scores - peak), 0.0)
    total = jnp.sum(pool_w, axis=0, keepdims=True) + jnp.sum(new_w, axis=0, keepdims=True)
    mixed = sum(dot(part, pool_v[...]) for part in split(pool_w.T, 3))
    tall_w = jnp.concatenate([new_w, jnp.zeros((lanes - 8, lanes), f32)], axis=0).T
    tall_v = jnp.concatenate([dv_ref[...], jnp.zeros((lanes - 8, cols), f32)], axis=0)
    mixed = mixed + exact_dot(tall_w, tall_v)
    mixed_ref[: half * each, :] = mixed[: half * each, :HD]
    mixed_ref[half * each : rows_used, :] = mixed[half * each : rows_used, HD:]
    state_ref[0:1, :] = peak
    state_ref[1:2, :] = total
    state_ref[2:, :] = jnp.zeros((6, lanes), f32)


def received_kernel(terms_ref, state_ref, mixed_ref, recv_ref, out_ref):
    lanes = terms_ref.shape[1]
    cols = terms_ref.shape[2]
    rows_used = mixed_ref.shape[0]
    half = rows_used // 2
    recv_rows = recv_ref.shape[0]
    keys = recv_ref[:, :cols]
    wide = dot(keys, terms_ref[...].reshape(3 * lanes, cols), NT)
    scores = (wide[:, :lanes] + wide[:, lanes : 2 * lanes] + wide[:, 2 * lanes :]) * SCALE
    valid = jnp.broadcast_to(keys[:, 0:1].astype(f32) < 0.5 * ABSENT, (recv_rows, lanes))
    before = state_ref[0:1, :]
    peak = jnp.maximum(
        before, jnp.max(jnp.where(valid, scores, FLOOR), axis=0, keepdims=True)
    )
    weights = jnp.where(valid, jnp.exp(scores - peak), 0.0)
    factor = jnp.exp(before - peak)
    total = state_ref[1:2, :] * factor + jnp.sum(weights, axis=0, keepdims=True)
    tall = dot(jnp.concatenate(split(weights.T, 2), axis=0), recv_ref[:, cols:])
    mixed = tall[:lanes] + tall[lanes:]
    kept = mixed_ref[...] * down(factor, rows_used)
    out_ref[:half, :] = (kept[:half] + mixed[:half, :HD]).astype(bf16)
    out_ref[half:rows_used, :] = (kept[half:] + mixed[half:rows_used, HD:]).astype(bf16)
    exact = [part.astype(f32) for part in split(peak, 3) + split(total, 3)]
    tail = jnp.concatenate(exact + [jnp.zeros((TAIL - len(exact), lanes), f32)], axis=0)
    out_ref[rows_used:, :] = tail.astype(bf16)


def finish_kernel(all_ref, w_ref, out_ref, attention):
    count = all_ref.shape[0]
    heads = attention.shape[1] // HD
    rows_used = all_ref.shape[1] - TAIL
    each = rows_used // heads
    tails = [all_ref[s, rows_used:, :].astype(f32) for s in range(count)]
    peaks = jnp.concatenate([t[0:1] + t[1:2] + t[2:3] for t in tails], axis=0)
    totals = jnp.concatenate([t[3:4] + t[4:5] + t[5:6] for t in tails], axis=0)
    factor = jnp.exp(peaks - jnp.max(peaks, axis=0, keepdims=True))
    share = factor / jnp.sum(factor * totals, axis=0, keepdims=True)
    share = jnp.concatenate([share, jnp.zeros((HD - count, HD), f32)], axis=0).T[:rows_used]
    mixed = share[:, 0:1] * all_ref[0, :rows_used, :].astype(f32)
    for s in range(1, count):
        mixed = mixed + share[:, s : s + 1] * all_ref[s, :rows_used, :].astype(f32)
    attention[...] = jnp.zeros_like(attention)
    for h in range(heads):
        attention[:each, h * HD : (h + 1) * HD] = mixed[h * each : (h + 1) * each, :]
    w = w_ref[...]
    terms = jnp.concatenate([part.astype(f32) for part in split(attention[...], 3)], axis=0)
    tall = dot(terms.astype(bf16), w)
    result = tall[:8] + tall[8:16] + tall[16:]
    pair = out_ref.shape[1]
    for n in range(out_ref.shape[0]):
        out_ref[n] = result[n * pair : (n + 1) * pair, :]


def prefill_kernel(seq_ref, q_hbm, kv_hbm, out_ref, q_ref, kv_ref, sems):
    seq = seq_ref[0]
    tokens = q_ref.shape[0]
    heads = q_ref.shape[1] // HD
    span = kv_ref.shape[0]
    group = heads // 2
    columns = [slice(i * HD, (i + 1) * HD) for i in range(4)]
    def attend(low, width):
        chunk = min(CHUNK, width - low)
        copies = [
            pltpu.make_async_copy(q_hbm, q_ref, sems.at[0]),
            pltpu.make_async_copy(kv_hbm.at[:width], kv_ref.at[:width], sems.at[1]),
        ]
        for copy in copies:
            copy.start()
        for copy in copies:
            copy.wait()
        q_at = lax.broadcasted_iota(jnp.int32, (2 * tokens, width - low), 0) % tokens + seq * tokens
        k_at = lax.broadcasted_iota(jnp.int32, (2 * tokens, width - low), 1) + low
        visible = k_at <= q_at

        def scores_of(pair):
            k = 2 * pair // group
            q = jnp.concatenate(
                [q_ref[:, h * HD : (h + 1) * HD] for h in (2 * pair, 2 * pair + 1)], axis=0
            )
            blocks = []
            for c in range(0, width, chunk):
                s = dot(q, kv_ref[c : c + chunk, columns[k]], NT)
                if c >= low:
                    s = jnp.where(visible[:, c - low : c - low + chunk], s, FLOOR)
                blocks.append(s)
            return blocks

        def finish(pair, blocks):
            k = 2 * pair // group
            peak = blocks[0]
            for s in blocks[1:]:
                peak = jnp.maximum(peak, s)
            peak = jnp.max(peak, axis=1, keepdims=True)
            mixed, total = None, None
            for i, s in enumerate(blocks):
                p = jnp.exp2((s - peak) * (SCALE * LOG2E))
                part = dot(p.astype(bf16), kv_ref[i * chunk : (i + 1) * chunk, columns[2 + k]])
                mixed = part if mixed is None else mixed + part
                total = p if total is None else total + p
            result = (mixed / jnp.sum(total, axis=1, keepdims=True)).astype(bf16)
            for n, h in enumerate((2 * pair, 2 * pair + 1)):
                out_ref[:, h * HD : (h + 1) * HD] = result[n * tokens : (n + 1) * tokens, :]

        now = scores_of(0)
        for pair in range(heads // 2):
            later = scores_of(pair + 1) if pair + 1 < heads // 2 else None
            finish(pair, now)
            now = later

    low, width = 0, 2 * tokens
    while low < span:
        inside = (seq * tokens >= low) & (seq * tokens < width)
        pl.when(inside)(lambda low=low, width=width: attend(low, width))
        low, width = width, width + min(width, CHUNK)


def local(
    pre_q, pre_k, pre_v, owner_map, cache_k, cache_v, tables, lengths, dec_q, dec_k, dec_v, w_out
):
    seq = lax.axis_index(SEQ).astype(jnp.int32).reshape(1)
    owners = lax.axis_size(BATCH)
    swap = [(0, 1), (1, 0)]
    tokens, cols = pre_k.shape[1], pre_k.shape[2]
    requests, new, q_cols = dec_q.shape
    rows_used = q_cols // HD * requests * new
    small = pltpu.CompilerParams(vmem_limit_bytes=16 * MIB)

    def rows8(x):
        x = x.transpose(1, 0, 2).reshape(requests * new, x.shape[-1])
        return jnp.pad(x, ((0, 8 - requests * new), (0, 0)))

    send, kv = pl.pallas_call(
        pack_kernel,
        out_shape=(
            jax.ShapeDtypeStruct((owners, SLOTS * PAGE, 2 * cols), bf16),
            jax.ShapeDtypeStruct((tokens, 2 * cols), bf16),
        ),
        in_specs=[SMEM, VMEM, VMEM],
        out_specs=(VMEM, VMEM),
        name="pack_pages",
    )(owner_map.reshape(-1), pre_k[0], pre_v[0])
    received = lax.all_to_all(send, BATCH, 0, 0, tiled=True)

    all_kv = lax.all_gather(kv, SEQ, axis=0, tiled=True)
    entries = tables.shape[1]
    terms, state, mixed = pl.pallas_call(
        cached_kernel,
        out_shape=(
            jax.ShapeDtypeStruct((3, HD, 2 * HD), bf16),
            jax.ShapeDtypeStruct((8, HD), f32),
            jax.ShapeDtypeStruct((rows_used, HD), f32),
        ),
        in_specs=[SMEM, SMEM, SMEM] + [VMEM] * 5,
        out_specs=(VMEM, VMEM, VMEM),
        scratch_shapes=[
            pltpu.VMEM((HD, 2 * HD), f32),
            pltpu.VMEM((requests * entries * PAGE, cols), bf16),
            pltpu.VMEM((requests * entries * PAGE, cols), bf16),
        ],
        compiler_params=small,
        name="cached_partial",
    )(
        seq, tables, lengths, rows8(dec_q), cache_k, cache_v,
        rows8(dec_k), rows8(dec_v),
    )
    partial_state = pl.pallas_call(
        received_kernel,
        out_shape=jax.ShapeDtypeStruct((rows_used + TAIL, HD), bf16),
        in_specs=[VMEM] * 4,
        out_specs=VMEM,
        compiler_params=small,
        name="received_partial",
    )(terms, state, mixed, received.reshape(owners * SLOTS * PAGE, 2 * cols))
    gathered = lax.all_gather(partial_state, SEQ)
    mine = pl.pallas_call(
        finish_kernel,
        out_shape=jax.ShapeDtypeStruct((new, requests, w_out.shape[1]), f32),
        in_specs=[VMEM, VMEM],
        out_specs=VMEM,
        scratch_shapes=[pltpu.VMEM((8, q_cols), f32)],
        compiler_params=small,
        name="finish_decode",
    )(gathered, w_out)
    other = lax.ppermute(mine, "tp", swap)

    group = q_cols // HD // 2
    span = all_kv.shape[0]
    pre_q, all_kv, mine = lax.optimization_barrier((pre_q, all_kv, mine))
    pre_out = pl.pallas_call(
        prefill_kernel,
        out_shape=jax.ShapeDtypeStruct((tokens, q_cols), bf16),
        in_specs=[SMEM, ANY, ANY],
        out_specs=VMEM,
        scratch_shapes=[
            pltpu.VMEM((tokens, q_cols), bf16),
            pltpu.VMEM((span, 2 * cols), bf16),
            pltpu.SemaphoreType.DMA((2,)),
        ],
        compiler_params=pltpu.CompilerParams(vmem_limit_bytes=60 * MIB),
        cost_estimate=pl.CostEstimate(
            flops=8 * group * tokens * span * HD,
            bytes_accessed=4 * MIB,
            transcendentals=2 * group * tokens * span,
        ),
        name="prefill_attention",
    )(seq, pre_q[0], all_kv)
    pre_out, other = lax.optimization_barrier((pre_out, other))
    dec_out = (mine + other).transpose(1, 0, 2)
    return (pre_out[None], dec_out)


def solution(mesh):
    cut = Mesh(mesh.devices.reshape(8, 2, 4, 4, 2), ("z", "core", "y", "x", "tp"))
    placed = (
        P(BATCH, SEQ, "tp"),
        P(BATCH, SEQ, "tp"),
        P(BATCH, SEQ, "tp"),
        P(BATCH, SEQ, None),
        P(BATCH, SEQ, "tp"),
        P(BATCH, SEQ, "tp"),
        P(BATCH, SEQ),
        P(BATCH),
        P(BATCH, None, "tp"),
        P(BATCH, None, "tp"),
        P(BATCH, None, "tp"),
        P("tp", SEQ),
    )
    return jax.shard_map(
        local,
        mesh=cut,
        in_specs=placed,
        out_specs=(P(BATCH, SEQ, "tp"), P(BATCH, None, SEQ)),
        check_vma=False,
    )
```

```python
import jax
import jax.numpy as jnp
from jax import lax
from jax.experimental import pallas as pl
from jax.experimental.pallas import tpu as pltpu
from jax.sharding import Mesh
from jax.sharding import PartitionSpec as P

HD = 128
PAGE = 16
NEW = 3
SLOTS = 2
CHUNK = 512
TAIL = 16
FLOOR = -1e30
SCALE = HD ** (-0.5)
LOG2E = 1.4426950408889634
ABSENT = 1024.0

SEQ = ("z", "core")
BATCH = ("y", "x")

f32 = jnp.float32
bf16 = jnp.bfloat16
MIB = 1024 * 1024
VMEM = pl.BlockSpec(memory_space=pltpu.VMEM)
SMEM = pl.BlockSpec(memory_space=pltpu.SMEM)
ANY = pl.BlockSpec(memory_space=pl.ANY)
NT = (((1,), (1,)), ((), ()))
NN = (((1,), (0,)), ((), ()))


def dot(a, b, dims=NN):
    return lax.dot_general(a, b, dims, preferred_element_type=f32)


def exact_dot(a, b, dims=NN):
    return lax.dot_general(
        a, b, dims, precision=lax.Precision.HIGHEST, preferred_element_type=f32
    )


def split(x, terms):
    out = []
    for _ in range(terms):
        part = x.astype(bf16)
        out.append(part)
        x = x - part.astype(f32)
    return out


def down(row, count):
    return jnp.broadcast_to(row, (row.shape[1], row.shape[1])).T[:count]


def pack_kernel(owner_ref, k_ref, v_ref, send_ref, kv_ref):
    cols = k_ref.shape[1]
    pages = k_ref.shape[0] // PAGE
    send_ref[:, :, :cols] = jnp.full((send_ref.shape[0], SLOTS * PAGE, cols), ABSENT, bf16)
    send_ref[:, :, cols:] = jnp.zeros((send_ref.shape[0], SLOTS * PAGE, cols), bf16)
    kv_ref[:, :cols] = k_ref[...]
    kv_ref[:, cols:] = v_ref[...]
    owners = [owner_ref[j] for j in range(pages)]
    for j in range(pages):
        slot = jnp.int32(0)
        for i in range(j):
            slot = slot + (owners[i] == owners[j]).astype(jnp.int32)
        slot = jnp.minimum(slot, SLOTS - 1)
        rows = pl.ds(pl.multiple_of(slot * PAGE, PAGE), PAGE)
        send_ref[owners[j], rows, :cols] = k_ref[j * PAGE : (j + 1) * PAGE, :]
        send_ref[owners[j], rows, cols:] = v_ref[j * PAGE : (j + 1) * PAGE, :]


def cached_kernel(
    seq_ref, table_ref, length_ref, q_ref, ck_ref, cv_ref, dk_ref, dv_ref,
    terms_ref, state_ref, mixed_ref, q_wide, pool_k, pool_v,
):
    seq = seq_ref[0]
    heads = q_ref.shape[1] // HD
    half = heads // 2
    requests, entries = table_ref.shape
    each = requests * NEW
    rows_used = heads * each
    lanes = q_wide.shape[0]
    cols = ck_ref.shape[2]
    q_wide[...] = jnp.zeros_like(q_wide)
    for h in range(heads):
        at = (h // half) * HD
        q_wide[h * each : (h + 1) * each, at : at + HD] = q_ref[:each, h * HD : (h + 1) * HD]
    for r in range(requests):
        for j in range(entries):
            rows = slice((r * entries + j) * PAGE, (r * entries + j + 1) * PAGE)
            page = table_ref[r, j]
            pool_k[rows, :] = ck_ref[page]
            pool_v[rows, :] = cv_ref[page]
    terms = split(q_wide[...], 3)
    for i, part in enumerate(terms):
        terms_ref[i] = part
    pool_scores = sum(dot(pool_k[...], part, NT) for part in terms) * SCALE
    pool_rows = requests * entries * PAGE
    key_at = lax.broadcasted_iota(jnp.int32, (pool_rows, lanes), 0)
    lane = lax.broadcasted_iota(jnp.int32, (pool_rows, lanes), 1)
    lane_request = lane % requests
    key_request = key_at // (entries * PAGE)
    local_at = key_at % (entries * PAGE)
    position = ((local_at // PAGE) * 16 + seq) * PAGE + local_at % PAGE
    length = jnp.where(key_request == 0, length_ref[0], length_ref[1])
    pool_valid = (position < length) & (lane_request == key_request)
    new_at = lax.broadcasted_iota(jnp.int32, (8, lanes), 0)
    new_lane = lax.broadcasted_iota(jnp.int32, (8, lanes), 1) % each
    new_valid = (
        (new_at < each)
        & (new_at % requests == new_lane % requests)
        & (new_at // requests <= new_lane // requests)
        & (seq == 0)
    )
    new_scores = exact_dot(dk_ref[...], q_wide[...], NT) * SCALE
    peak = jnp.maximum(
        jnp.max(jnp.where(pool_valid, pool_scores, FLOOR), axis=0, keepdims=True),
        jnp.max(jnp.where(new_valid, new_scores, FLOOR), axis=0, keepdims=True),
    )
    pool_w = jnp.where(pool_valid, jnp.exp(pool_scores - peak), 0.0)
    new_w = jnp.where(new_valid, jnp.exp(new_scores - peak), 0.0)
    total = jnp.sum(pool_w, axis=0, keepdims=True) + jnp.sum(new_w, axis=0, keepdims=True)
    mixed = sum(dot(part, pool_v[...]) for part in split(pool_w.T, 3))
    tall_w = jnp.concatenate([new_w, jnp.zeros((lanes - 8, lanes), f32)], axis=0).T
    tall_v = jnp.concatenate([dv_ref[...], jnp.zeros((lanes - 8, cols), f32)], axis=0)
    mixed = mixed + exact_dot(tall_w, tall_v)
    mixed_ref[: half * each, :] = mixed[: half * each, :HD]
    mixed_ref[half * each : rows_used, :] = mixed[half * each : rows_used, HD:]
    state_ref[0:1, :] = peak
    state_ref[1:2, :] = total
    state_ref[2:, :] = jnp.zeros((6, lanes), f32)


def received_kernel(terms_ref, state_ref, mixed_ref, recv_ref, out_ref):
    lanes = terms_ref.shape[1]
    cols = terms_ref.shape[2]
    rows_used = mixed_ref.shape[0]
    half = rows_used // 2
    recv_rows = recv_ref.shape[0]
    keys = recv_ref[:, :cols]
    wide = dot(keys, terms_ref[...].reshape(3 * lanes, cols), NT)
    scores = (wide[:, :lanes] + wide[:, lanes : 2 * lanes] + wide[:, 2 * lanes :]) * SCALE
    valid = jnp.broadcast_to(keys[:, 0:1].astype(f32) < 0.5 * ABSENT, (recv_rows, lanes))
    before = state_ref[0:1, :]
    peak = jnp.maximum(
        before, jnp.max(jnp.where(valid, scores, FLOOR), axis=0, keepdims=True)
    )
    weights = jnp.where(valid, jnp.exp(scores - peak), 0.0)
    factor = jnp.exp(before - peak)
    total = state_ref[1:2, :] * factor + jnp.sum(weights, axis=0, keepdims=True)
    tall = dot(jnp.concatenate(split(weights.T, 2), axis=0), recv_ref[:, cols:])
    mixed = tall[:lanes] + tall[lanes:]
    kept = mixed_ref[...] * down(factor, rows_used)
    out_ref[:half, :] = (kept[:half] + mixed[:half, :HD]).astype(bf16)
    out_ref[half:rows_used, :] = (kept[half:] + mixed[half:rows_used, HD:]).astype(bf16)
    exact = [part.astype(f32) for part in split(peak, 3) + split(total, 3)]
    tail = jnp.concatenate(exact + [jnp.zeros((TAIL - len(exact), lanes), f32)], axis=0)
    out_ref[rows_used:, :] = tail.astype(bf16)


def finish_kernel(all_ref, w_ref, out_ref, attention):
    count = all_ref.shape[0]
    heads = attention.shape[1] // HD
    rows_used = all_ref.shape[1] - TAIL
    each = rows_used // heads
    tails = [all_ref[s, rows_used:, :].astype(f32) for s in range(count)]
    peaks = jnp.concatenate([t[0:1] + t[1:2] + t[2:3] for t in tails], axis=0)
    totals = jnp.concatenate([t[3:4] + t[4:5] + t[5:6] for t in tails], axis=0)
    factor = jnp.exp(peaks - jnp.max(peaks, axis=0, keepdims=True))
    share = factor / jnp.sum(factor * totals, axis=0, keepdims=True)
    share = jnp.concatenate([share, jnp.zeros((HD - count, HD), f32)], axis=0).T[:rows_used]
    mixed = share[:, 0:1] * all_ref[0, :rows_used, :].astype(f32)
    for s in range(1, count):
        mixed = mixed + share[:, s : s + 1] * all_ref[s, :rows_used, :].astype(f32)
    attention[...] = jnp.zeros_like(attention)
    for h in range(heads):
        attention[:each, h * HD : (h + 1) * HD] = mixed[h * each : (h + 1) * each, :]
    w = w_ref[...]
    terms = jnp.concatenate([part.astype(f32) for part in split(attention[...], 3)], axis=0)
    tall = dot(terms.astype(bf16), w)
    result = tall[:8] + tall[8:16] + tall[16:]
    pair = out_ref.shape[1]
    for n in range(out_ref.shape[0]):
        out_ref[n] = result[n * pair : (n + 1) * pair, :]


def prefill_kernel(seq_ref, q_hbm, kv_hbm, out_ref, q_ref, kv_ref, sems):
    seq = seq_ref[0]
    tokens = q_ref.shape[0]
    heads = q_ref.shape[1] // HD
    span = kv_ref.shape[0]
    group = heads // 2
    columns = [slice(i * HD, (i + 1) * HD) for i in range(4)]
    def attend(low, width):
        chunk = min(CHUNK, width - low)
        copies = [
            pltpu.make_async_copy(q_hbm, q_ref, sems.at[0]),
            pltpu.make_async_copy(kv_hbm.at[:width], kv_ref.at[:width], sems.at[1]),
        ]
        for copy in copies:
            copy.start()
        for copy in copies:
            copy.wait()
        q_at = lax.broadcasted_iota(jnp.int32, (2 * tokens, width - low), 0) % tokens + seq * tokens
        k_at = lax.broadcasted_iota(jnp.int32, (2 * tokens, width - low), 1) + low
        visible = k_at <= q_at

        def scores_of(pair):
            k = 2 * pair // group
            q = jnp.concatenate(
                [q_ref[:, h * HD : (h + 1) * HD] for h in (2 * pair, 2 * pair + 1)], axis=0
            )
            blocks = []
            for c in range(0, width, chunk):
                s = dot(q, kv_ref[c : c + chunk, columns[k]], NT)
                if c >= low:
                    s = jnp.where(visible[:, c - low : c - low + chunk], s, FLOOR)
                blocks.append(s)
            return blocks

        def finish(pair, blocks):
            k = 2 * pair // group
            peak = blocks[0]
            for s in blocks[1:]:
                peak = jnp.maximum(peak, s)
            peak = jnp.max(peak, axis=1, keepdims=True)
            mixed, total = None, None
            for i, s in enumerate(blocks):
                p = jnp.exp2((s - peak) * (SCALE * LOG2E))
                part = dot(p.astype(bf16), kv_ref[i * chunk : (i + 1) * chunk, columns[2 + k]])
                mixed = part if mixed is None else mixed + part
                total = p if total is None else total + p
            result = (mixed / jnp.sum(total, axis=1, keepdims=True)).astype(bf16)
            for n, h in enumerate((2 * pair, 2 * pair + 1)):
                out_ref[:, h * HD : (h + 1) * HD] = result[n * tokens : (n + 1) * tokens, :]

        now = scores_of(0)
        for pair in range(heads // 2):
            later = scores_of(pair + 1) if pair + 1 < heads // 2 else None
            finish(pair, now)
            now = later

    low, width = 0, 2 * tokens
    while low < span:
        inside = (seq * tokens >= low) & (seq * tokens < width)
        pl.when(inside)(lambda low=low, width=width: attend(low, width))
        low, width = width, width + min(width, CHUNK)


def local(
    pre_q, pre_k, pre_v, owner_map, cache_k, cache_v, tables, lengths, dec_q, dec_k, dec_v, w_out
):
    seq = lax.axis_index(SEQ).astype(jnp.int32).reshape(1)
    owners = lax.axis_size(BATCH)
    swap = [(0, 1), (1, 0)]
    tokens, cols = pre_k.shape[1], pre_k.shape[2]
    requests, new, q_cols = dec_q.shape
    rows_used = q_cols // HD * requests * new
    small = pltpu.CompilerParams(vmem_limit_bytes=16 * MIB)

    def rows8(x):
        x = x.transpose(1, 0, 2).reshape(requests * new, x.shape[-1])
        return jnp.pad(x, ((0, 8 - requests * new), (0, 0)))

    send, kv = pl.pallas_call(
        pack_kernel,
        out_shape=(
            jax.ShapeDtypeStruct((owners, SLOTS * PAGE, 2 * cols), bf16),
            jax.ShapeDtypeStruct((tokens, 2 * cols), bf16),
        ),
        in_specs=[SMEM, VMEM, VMEM],
        out_specs=(VMEM, VMEM),
        name="pack_pages",
    )(owner_map.reshape(-1), pre_k[0], pre_v[0])
    received = lax.all_to_all(send, BATCH, 0, 0, tiled=True)

    all_kv = lax.all_gather(kv, SEQ, axis=0, tiled=True)
    entries = tables.shape[1]
    terms, state, mixed = pl.pallas_call(
        cached_kernel,
        out_shape=(
            jax.ShapeDtypeStruct((3, HD, 2 * HD), bf16),
            jax.ShapeDtypeStruct((8, HD), f32),
            jax.ShapeDtypeStruct((rows_used, HD), f32),
        ),
        in_specs=[SMEM, SMEM, SMEM] + [VMEM] * 5,
        out_specs=(VMEM, VMEM, VMEM),
        scratch_shapes=[
            pltpu.VMEM((HD, 2 * HD), f32),
            pltpu.VMEM((requests * entries * PAGE, cols), bf16),
            pltpu.VMEM((requests * entries * PAGE, cols), bf16),
        ],
        compiler_params=small,
        name="cached_partial",
    )(
        seq, tables, lengths, rows8(dec_q), cache_k, cache_v,
        rows8(dec_k), rows8(dec_v),
    )
    partial_state = pl.pallas_call(
        received_kernel,
        out_shape=jax.ShapeDtypeStruct((rows_used + TAIL, HD), bf16),
        in_specs=[VMEM] * 4,
        out_specs=VMEM,
        compiler_params=small,
        name="received_partial",
    )(terms, state, mixed, received.reshape(owners * SLOTS * PAGE, 2 * cols))
    copies = jnp.broadcast_to(partial_state[None], (lax.axis_size(SEQ), *partial_state.shape))
    gathered = lax.all_to_all(copies, SEQ, 0, 0, tiled=True)
    mine = pl.pallas_call(
        finish_kernel,
        out_shape=jax.ShapeDtypeStruct((new, requests, w_out.shape[1]), f32),
        in_specs=[VMEM, VMEM],
        out_specs=VMEM,
        scratch_shapes=[pltpu.VMEM((8, q_cols), f32)],
        compiler_params=small,
        name="finish_decode",
    )(gathered, w_out)
    other = lax.ppermute(mine, "tp", swap)

    group = q_cols // HD // 2
    span = all_kv.shape[0]
    pre_q, all_kv, mine = lax.optimization_barrier((pre_q, all_kv, mine))
    pre_out = pl.pallas_call(
        prefill_kernel,
        out_shape=jax.ShapeDtypeStruct((tokens, q_cols), bf16),
        in_specs=[SMEM, ANY, ANY],
        out_specs=VMEM,
        scratch_shapes=[
            pltpu.VMEM((tokens, q_cols), bf16),
            pltpu.VMEM((span, 2 * cols), bf16),
            pltpu.SemaphoreType.DMA((2,)),
        ],
        compiler_params=pltpu.CompilerParams(vmem_limit_bytes=60 * MIB),
        cost_estimate=pl.CostEstimate(
            flops=8 * group * tokens * span * HD,
            bytes_accessed=4 * MIB,
            transcendentals=2 * group * tokens * span,
        ),
        name="prefill_attention",
    )(seq, pre_q[0], all_kv)
    pre_out, other = lax.optimization_barrier((pre_out, other))
    dec_out = (mine + other).transpose(1, 0, 2)
    return (pre_out[None], dec_out)


def solution(mesh):
    cut = Mesh(mesh.devices.reshape(8, 2, 4, 4, 2), ("z", "core", "y", "x", "tp"))
    placed = (
        P(BATCH, SEQ, "tp"),
        P(BATCH, SEQ, "tp"),
        P(BATCH, SEQ, "tp"),
        P(BATCH, SEQ, None),
        P(BATCH, SEQ, "tp"),
        P(BATCH, SEQ, "tp"),
        P(BATCH, SEQ),
        P(BATCH),
        P(BATCH, None, "tp"),
        P(BATCH, None, "tp"),
        P(BATCH, None, "tp"),
        P("tp", SEQ),
    )
    return jax.shard_map(
        local,
        mesh=cut,
        in_specs=placed,
        out_specs=(P(BATCH, SEQ, "tp"), P(BATCH, None, SEQ)),
        check_vma=False,
    )
```

```python
import jax
import jax.numpy as jnp
from jax import lax
from jax.experimental import pallas as pl
from jax.experimental.pallas import tpu as pltpu
from jax.sharding import Mesh
from jax.sharding import PartitionSpec as P

HD = 128
PAGE = 16
NEW = 3
SLOTS = 2
CHUNK = 512
TAIL = 16
FLOOR = -1e30
SCALE = HD ** (-0.5)
LOG2E = 1.4426950408889634
ABSENT = 1024.0

SEQ = ("z", "core")
BATCH = ("y", "x")

f32 = jnp.float32
bf16 = jnp.bfloat16
MIB = 1024 * 1024
VMEM = pl.BlockSpec(memory_space=pltpu.VMEM)
SMEM = pl.BlockSpec(memory_space=pltpu.SMEM)
ANY = pl.BlockSpec(memory_space=pl.ANY)
NT = (((1,), (1,)), ((), ()))
NN = (((1,), (0,)), ((), ()))


def dot(a, b, dims=NN):
    return lax.dot_general(a, b, dims, preferred_element_type=f32)


def exact_dot(a, b, dims=NN):
    return lax.dot_general(
        a, b, dims, precision=lax.Precision.HIGHEST, preferred_element_type=f32
    )


def split(x, terms):
    out = []
    for _ in range(terms):
        part = x.astype(bf16)
        out.append(part)
        x = x - part.astype(f32)
    return out


def down(row, count):
    return jnp.broadcast_to(row, (row.shape[1], row.shape[1])).T[:count]


def pack_kernel(owner_ref, k_ref, v_ref, send_ref, kv_ref):
    cols = k_ref.shape[1]
    pages = k_ref.shape[0] // PAGE
    send_ref[:, :, :cols] = jnp.full((send_ref.shape[0], SLOTS * PAGE, cols), ABSENT, bf16)
    send_ref[:, :, cols:] = jnp.zeros((send_ref.shape[0], SLOTS * PAGE, cols), bf16)
    kv_ref[:, :cols] = k_ref[...]
    kv_ref[:, cols:] = v_ref[...]
    owners = [owner_ref[j] for j in range(pages)]
    for j in range(pages):
        slot = jnp.int32(0)
        for i in range(j):
            slot = slot + (owners[i] == owners[j]).astype(jnp.int32)
        slot = jnp.minimum(slot, SLOTS - 1)
        rows = pl.ds(pl.multiple_of(slot * PAGE, PAGE), PAGE)
        send_ref[owners[j], rows, :cols] = k_ref[j * PAGE : (j + 1) * PAGE, :]
        send_ref[owners[j], rows, cols:] = v_ref[j * PAGE : (j + 1) * PAGE, :]


def cached_kernel(
    seq_ref, table_ref, length_ref, q_ref, ck_ref, cv_ref, dk_ref, dv_ref,
    terms_ref, state_ref, mixed_ref, q_wide, pool_k, pool_v,
):
    seq = seq_ref[0]
    heads = q_ref.shape[1] // HD
    half = heads // 2
    requests, entries = table_ref.shape
    each = requests * NEW
    rows_used = heads * each
    lanes = q_wide.shape[0]
    cols = ck_ref.shape[2]
    q_wide[...] = jnp.zeros_like(q_wide)
    for h in range(heads):
        at = (h // half) * HD
        q_wide[h * each : (h + 1) * each, at : at + HD] = q_ref[:each, h * HD : (h + 1) * HD]
    for r in range(requests):
        for j in range(entries):
            rows = slice((r * entries + j) * PAGE, (r * entries + j + 1) * PAGE)
            page = table_ref[r, j]
            pool_k[rows, :] = ck_ref[page]
            pool_v[rows, :] = cv_ref[page]
    terms = split(q_wide[...], 3)
    for i, part in enumerate(terms):
        terms_ref[i] = part
    pool_scores = sum(dot(pool_k[...], part, NT) for part in terms) * SCALE
    pool_rows = requests * entries * PAGE
    key_at = lax.broadcasted_iota(jnp.int32, (pool_rows, lanes), 0)
    lane = lax.broadcasted_iota(jnp.int32, (pool_rows, lanes), 1)
    lane_request = lane % requests
    key_request = key_at // (entries * PAGE)
    local_at = key_at % (entries * PAGE)
    position = ((local_at // PAGE) * 16 + seq) * PAGE + local_at % PAGE
    length = jnp.where(key_request == 0, length_ref[0], length_ref[1])
    pool_valid = (position < length) & (lane_request == key_request)
    new_at = lax.broadcasted_iota(jnp.int32, (8, lanes), 0)
    new_lane = lax.broadcasted_iota(jnp.int32, (8, lanes), 1) % each
    new_valid = (
        (new_at < each)
        & (new_at % requests == new_lane % requests)
        & (new_at // requests <= new_lane // requests)
        & (seq == 0)
    )
    new_scores = exact_dot(dk_ref[...], q_wide[...], NT) * SCALE
    peak = jnp.maximum(
        jnp.max(jnp.where(pool_valid, pool_scores, FLOOR), axis=0, keepdims=True),
        jnp.max(jnp.where(new_valid, new_scores, FLOOR), axis=0, keepdims=True),
    )
    pool_w = jnp.where(pool_valid, jnp.exp(pool_scores - peak), 0.0)
    new_w = jnp.where(new_valid, jnp.exp(new_scores - peak), 0.0)
    total = jnp.sum(pool_w, axis=0, keepdims=True) + jnp.sum(new_w, axis=0, keepdims=True)
    mixed = sum(dot(part, pool_v[...]) for part in split(pool_w.T, 3))
    tall_w = jnp.concatenate([new_w, jnp.zeros((lanes - 8, lanes), f32)], axis=0).T
    tall_v = jnp.concatenate([dv_ref[...], jnp.zeros((lanes - 8, cols), f32)], axis=0)
    mixed = mixed + exact_dot(tall_w, tall_v)
    mixed_ref[: half * each, :] = mixed[: half * each, :HD]
    mixed_ref[half * each : rows_used, :] = mixed[half * each : rows_used, HD:]
    state_ref[0:1, :] = peak
    state_ref[1:2, :] = total
    state_ref[2:, :] = jnp.zeros((6, lanes), f32)


def received_kernel(terms_ref, state_ref, mixed_ref, recv_ref, out_ref):
    lanes = terms_ref.shape[1]
    cols = terms_ref.shape[2]
    rows_used = mixed_ref.shape[0]
    half = rows_used // 2
    recv_rows = recv_ref.shape[0]
    keys = recv_ref[:, :cols]
    wide = dot(keys, terms_ref[...].reshape(3 * lanes, cols), NT)
    scores = (wide[:, :lanes] + wide[:, lanes : 2 * lanes] + wide[:, 2 * lanes :]) * SCALE
    valid = jnp.broadcast_to(keys[:, 0:1].astype(f32) < 0.5 * ABSENT, (recv_rows, lanes))
    before = state_ref[0:1, :]
    peak = jnp.maximum(
        before, jnp.max(jnp.where(valid, scores, FLOOR), axis=0, keepdims=True)
    )
    weights = jnp.where(valid, jnp.exp(scores - peak), 0.0)
    factor = jnp.exp(before - peak)
    total = state_ref[1:2, :] * factor + jnp.sum(weights, axis=0, keepdims=True)
    tall = dot(jnp.concatenate(split(weights.T, 2), axis=0), recv_ref[:, cols:])
    mixed = tall[:lanes] + tall[lanes:]
    kept = mixed_ref[...] * down(factor, rows_used)
    out_ref[:half, :] = (kept[:half] + mixed[:half, :HD]).astype(bf16)
    out_ref[half:rows_used, :] = (kept[half:] + mixed[half:rows_used, HD:]).astype(bf16)
    exact = [part.astype(f32) for part in split(peak, 3) + split(total, 3)]
    tail = jnp.concatenate(exact + [jnp.zeros((TAIL - len(exact), lanes), f32)], axis=0)
    out_ref[rows_used:, :] = tail.astype(bf16)


def finish_kernel(all_ref, w_ref, out_ref, attention):
    count = all_ref.shape[0]
    heads = attention.shape[1] // HD
    rows_used = all_ref.shape[1] - TAIL
    each = rows_used // heads
    tails = [all_ref[s, rows_used:, :].astype(f32) for s in range(count)]
    peaks = jnp.concatenate([t[0:1] + t[1:2] + t[2:3] for t in tails], axis=0)
    totals = jnp.concatenate([t[3:4] + t[4:5] + t[5:6] for t in tails], axis=0)
    factor = jnp.exp(peaks - jnp.max(peaks, axis=0, keepdims=True))
    share = factor / jnp.sum(factor * totals, axis=0, keepdims=True)
    share = jnp.concatenate([share, jnp.zeros((HD - count, HD), f32)], axis=0).T[:rows_used]
    mixed = share[:, 0:1] * all_ref[0, :rows_used, :].astype(f32)
    for s in range(1, count):
        mixed = mixed + share[:, s : s + 1] * all_ref[s, :rows_used, :].astype(f32)
    attention[...] = jnp.zeros_like(attention)
    for h in range(heads):
        attention[:each, h * HD : (h + 1) * HD] = mixed[h * each : (h + 1) * each, :]
    w = w_ref[...]
    terms = jnp.concatenate([part.astype(f32) for part in split(attention[...], 2)], axis=0)
    tall = dot(terms.astype(bf16), w)
    result = tall[:8] + tall[8:]
    pair = out_ref.shape[1]
    for n in range(out_ref.shape[0]):
        out_ref[n] = result[n * pair : (n + 1) * pair, :]


def prefill_kernel(seq_ref, q_hbm, kv_hbm, out_ref, q_ref, kv_ref, sems):
    seq = seq_ref[0]
    tokens = q_ref.shape[0]
    heads = q_ref.shape[1] // HD
    span = kv_ref.shape[0]
    group = heads // 2
    columns = [slice(i * HD, (i + 1) * HD) for i in range(4)]
    def attend(low, width):
        chunk = min(CHUNK, width - low)
        copies = [
            pltpu.make_async_copy(q_hbm, q_ref, sems.at[0]),
            pltpu.make_async_copy(kv_hbm.at[:width], kv_ref.at[:width], sems.at[1]),
        ]
        for copy in copies:
            copy.start()
        for copy in copies:
            copy.wait()
        q_at = lax.broadcasted_iota(jnp.int32, (2 * tokens, width - low), 0) % tokens + seq * tokens
        k_at = lax.broadcasted_iota(jnp.int32, (2 * tokens, width - low), 1) + low
        visible = k_at <= q_at

        def scores_of(pair):
            k = 2 * pair // group
            q = jnp.concatenate(
                [q_ref[:, h * HD : (h + 1) * HD] for h in (2 * pair, 2 * pair + 1)], axis=0
            )
            blocks = []
            for c in range(0, width, chunk):
                s = dot(q, kv_ref[c : c + chunk, columns[k]], NT)
                if c >= low:
                    s = jnp.where(visible[:, c - low : c - low + chunk], s, FLOOR)
                blocks.append(s)
            return blocks

        def finish(pair, blocks):
            k = 2 * pair // group
            peak = blocks[0]
            for s in blocks[1:]:
                peak = jnp.maximum(peak, s)
            peak = jnp.max(peak, axis=1, keepdims=True)
            mixed, total = None, None
            for i, s in enumerate(blocks):
                p = jnp.exp2((s - peak) * (SCALE * LOG2E))
                part = dot(p.astype(bf16), kv_ref[i * chunk : (i + 1) * chunk, columns[2 + k]])
                mixed = part if mixed is None else mixed + part
                total = p if total is None else total + p
            result = (mixed / jnp.sum(total, axis=1, keepdims=True)).astype(bf16)
            for n, h in enumerate((2 * pair, 2 * pair + 1)):
                out_ref[:, h * HD : (h + 1) * HD] = result[n * tokens : (n + 1) * tokens, :]

        now = scores_of(0)
        for pair in range(heads // 2):
            later = scores_of(pair + 1) if pair + 1 < heads // 2 else None
            finish(pair, now)
            now = later

    low, width = 0, 2 * tokens
    while low < span:
        inside = (seq * tokens >= low) & (seq * tokens < width)
        pl.when(inside)(lambda low=low, width=width: attend(low, width))
        low, width = width, width + min(width, CHUNK)


def local(
    pre_q, pre_k, pre_v, owner_map, cache_k, cache_v, tables, lengths, dec_q, dec_k, dec_v, w_out
):
    seq = lax.axis_index(SEQ).astype(jnp.int32).reshape(1)
    owners = lax.axis_size(BATCH)
    swap = [(0, 1), (1, 0)]
    tokens, cols = pre_k.shape[1], pre_k.shape[2]
    requests, new, q_cols = dec_q.shape
    rows_used = q_cols // HD * requests * new
    small = pltpu.CompilerParams(vmem_limit_bytes=16 * MIB)

    def rows8(x):
        x = x.transpose(1, 0, 2).reshape(requests * new, x.shape[-1])
        return jnp.pad(x, ((0, 8 - requests * new), (0, 0)))

    send, kv = pl.pallas_call(
        pack_kernel,
        out_shape=(
            jax.ShapeDtypeStruct((owners, SLOTS * PAGE, 2 * cols), bf16),
            jax.ShapeDtypeStruct((tokens, 2 * cols), bf16),
        ),
        in_specs=[SMEM, VMEM, VMEM],
        out_specs=(VMEM, VMEM),
        name="pack_pages",
    )(owner_map.reshape(-1), pre_k[0], pre_v[0])
    received = lax.all_to_all(send, BATCH, 0, 0, tiled=True)

    all_kv = lax.all_gather(kv, SEQ, axis=0, tiled=True)
    entries = tables.shape[1]
    terms, state, mixed = pl.pallas_call(
        cached_kernel,
        out_shape=(
            jax.ShapeDtypeStruct((3, HD, 2 * HD), bf16),
            jax.ShapeDtypeStruct((8, HD), f32),
            jax.ShapeDtypeStruct((rows_used, HD), f32),
        ),
        in_specs=[SMEM, SMEM, SMEM] + [VMEM] * 5,
        out_specs=(VMEM, VMEM, VMEM),
        scratch_shapes=[
            pltpu.VMEM((HD, 2 * HD), f32),
            pltpu.VMEM((requests * entries * PAGE, cols), bf16),
            pltpu.VMEM((requests * entries * PAGE, cols), bf16),
        ],
        compiler_params=small,
        name="cached_partial",
    )(
        seq, tables, lengths, rows8(dec_q), cache_k, cache_v,
        rows8(dec_k), rows8(dec_v),
    )
    partial_state = pl.pallas_call(
        received_kernel,
        out_shape=jax.ShapeDtypeStruct((rows_used + TAIL, HD), bf16),
        in_specs=[VMEM] * 4,
        out_specs=VMEM,
        compiler_params=small,
        name="received_partial",
    )(terms, state, mixed, received.reshape(owners * SLOTS * PAGE, 2 * cols))
    gathered = lax.all_gather(partial_state, SEQ)
    mine = pl.pallas_call(
        finish_kernel,
        out_shape=jax.ShapeDtypeStruct((new, requests, w_out.shape[1]), f32),
        in_specs=[VMEM, VMEM],
        out_specs=VMEM,
        scratch_shapes=[pltpu.VMEM((8, q_cols), f32)],
        compiler_params=small,
        name="finish_decode",
    )(gathered, w_out)
    other = lax.ppermute(mine, "tp", swap)

    group = q_cols // HD // 2
    span = all_kv.shape[0]
    pre_q, all_kv, mine = lax.optimization_barrier((pre_q, all_kv, mine))
    pre_out = pl.pallas_call(
        prefill_kernel,
        out_shape=jax.ShapeDtypeStruct((tokens, q_cols), bf16),
        in_specs=[SMEM, ANY, ANY],
        out_specs=VMEM,
        scratch_shapes=[
            pltpu.VMEM((tokens, q_cols), bf16),
            pltpu.VMEM((span, 2 * cols), bf16),
            pltpu.SemaphoreType.DMA((2,)),
        ],
        compiler_params=pltpu.CompilerParams(vmem_limit_bytes=60 * MIB),
        cost_estimate=pl.CostEstimate(
            flops=8 * group * tokens * span * HD,
            bytes_accessed=4 * MIB,
            transcendentals=2 * group * tokens * span,
        ),
        name="prefill_attention",
    )(seq, pre_q[0], all_kv)
    pre_out, other = lax.optimization_barrier((pre_out, other))
    dec_out = (mine + other).transpose(1, 0, 2)
    return (pre_out[None], dec_out)


def solution(mesh):
    cut = Mesh(mesh.devices.reshape(8, 2, 4, 4, 2), ("z", "core", "y", "x", "tp"))
    placed = (
        P(BATCH, SEQ, "tp"),
        P(BATCH, SEQ, "tp"),
        P(BATCH, SEQ, "tp"),
        P(BATCH, SEQ, None),
        P(BATCH, SEQ, "tp"),
        P(BATCH, SEQ, "tp"),
        P(BATCH, SEQ),
        P(BATCH),
        P(BATCH, None, "tp"),
        P(BATCH, None, "tp"),
        P(BATCH, None, "tp"),
        P("tp", SEQ),
    )
    return jax.shard_map(
        local,
        mesh=cut,
        in_specs=placed,
        out_specs=(P(BATCH, SEQ, "tp"), P(BATCH, None, SEQ)),
        check_vma=False,
    )
```
